32 devices in a mesh: dp: 4 (over y, core), seq: 8 (over z, x).
Axes of the slice: x: 2, y: 2, z: 4, core: 2. Of those that a mesh axis runs over, the one named last changes fastest.
Arguments:
- region: bfloat16 [32, 512, 192], P(('dp', 'seq')), parts along dimension 0, may hold values from -11 to 11
- norm_gain: float32 [192], replicated, may hold values from 0.1 to 1.9
- in_weight: bfloat16 [192, 768], replicated, may hold values from -0.4375 to 0.4375
- conv_weight: float32 [9, 384], replicated, may hold values from -2 to 2
- conv_bias: float32 [384], replicated, may hold values from -3 to 3
- coupling_weight: bfloat16 [384, 512], replicated, may hold values from -0.3125 to 0.3125
- step_weight: bfloat16 [384, 24], replicated, may hold values from -0.3125 to 0.3125
- step_bias: float32 [24], replicated, may hold values from -1 to 1
- decay_log: float32 [24], replicated, may hold values from -16 to -2.9
- skip_gain: float32 [24], replicated, may hold values from 0.5 to 12
- out_gain: float32 [384], replicated, may hold values from 0.1 to 1.9
- out_weight: bfloat16 [384, 192], replicated, may hold values from -0.3125 to 0.3125
Outputs:
- refined: bfloat16 [32, 512, 192], P(('dp', 'seq')), parts along dimension 0
The draws below stay inside these ranges and needn't reach their ends.
There are 4 independent parts, one for each index of `dp`. The reference program is written for one: setup_inputs(seed, part) draws one part's arguments, and reference() takes and returns one part's arrays. A program takes and returns all parts, laid end to end along the dimension named above; an argument that names none is the same for every part. Nothing has to cross between parts.
All inputs are finite; a program needn't handle non-finite values.
Results may differ from the reference program's by a relative error of at most 0.0035.
The reference program's roundings to bfloat16 on the way count: a program that leaves them out, or rounds other values in their place, can miss the bound.
Values may be sent and summed in bfloat16 or wider, within the bound.
A program may use at most 128 MiB of HBM per device.

```python
import math
import jax
import jax.numpy as jnp
from jax import lax

WIDTH = 192
HEADS = 6
STATE = 64
INNER = 384
COLS = 512
BLOCK = 512
ROWS = 8


def draw_decay_log(key, part):
    pick_key, fast_key, middle_key, slow_key = jax.random.split(key, 4)
    entry_count = 4 * HEADS
    quick_share = 0.4
    middle_share = 0.3
    picked = jax.random.uniform(pick_key, (entry_count,))
    fast_rate = jnp.log(jax.random.uniform(fast_key, (entry_count,), minval=1.0 / 50.0, maxval=1.0 / 20.0))
    middle_rate = jax.random.uniform(middle_key, (entry_count,), minval=-6.5, maxval=-5.3)
    slow_rate = jnp.log(jax.random.uniform(slow_key, (entry_count,), minval=0.4, maxval=2.5) / (ROWS * COLS))
    chosen = jnp.where(picked < quick_share, fast_rate, jnp.where(picked < quick_share + middle_share, middle_rate, slow_rate))
    return chosen.astype(jnp.float32)


def draw_region(key, part):
    noise_key, direction_key, level_key, column_key, ramp_key, sign_key, rough_key = jax.random.split(key, 7)
    noise = jnp.clip(jax.random.normal(noise_key, (ROWS, COLS, WIDTH)), -6.0, 6.0)
    direction = jnp.clip(jax.random.normal(direction_key, (WIDTH,)), -3.0, 3.0)
    level = jax.random.uniform(level_key, (ROWS, 1, 1), minval=-1.5, maxval=1.5)
    column_direction = jnp.clip(jax.random.normal(column_key, (WIDTH,)), -3.0, 3.0)
    ramp_size = jax.random.uniform(ramp_key, (), minval=1.2, maxval=2.0)
    ramp_sign = jnp.where(jax.random.uniform(sign_key, ()) < 0.5, -1.0, 1.0)
    places = (2.0 * jnp.arange(COLS, dtype=jnp.float32) + 1.0) / COLS - 1.0
    rough = jnp.repeat(jax.random.uniform(rough_key, (COLS // 16,), minval=-0.5, maxval=0.5), 16)
    column_level = ramp_size * ramp_sign * places + rough
    values = noise + level * direction[None, None, :] + column_level[None, :, None] * column_direction[None, None, :]
    return jnp.clip(values, -11.0, 11.0).astype(jnp.float32).astype(jnp.bfloat16)


def centred(key, extent, scale, bound, kind=jnp.bfloat16):
    return jnp.clip(scale * jax.random.normal(key, extent, jnp.float32), -bound, bound).astype(kind)


def setup_inputs(seed: int = 0, part: int = 0) -> dict:
    key_list = jax.random.split(jax.random.key(seed), 13)
    part_splits = jax.random.split(jax.random.fold_in(key_list[12], part), 13)
    return {
        "region": draw_region(jax.random.fold_in(jax.random.fold_in(key_list[12], part), 71), part),
        "norm_gain": jnp.clip(1.0 + 0.18 * jax.random.normal(key_list[1], (WIDTH,), jnp.float32), 0.1, 1.9),
        "in_weight": centred(key_list[2], (WIDTH, 2 * INNER), WIDTH ** -0.5, 0.4375),
        "conv_weight": centred(key_list[3], (9, INNER), 9 ** -0.5, 2.0, jnp.float32),
        "conv_bias": centred(key_list[4], (INNER,), 0.5, 3.0, jnp.float32),
        "coupling_weight": centred(key_list[5], (INNER, 8 * STATE), INNER ** -0.5, 0.3125),
        "step_weight": centred(key_list[6], (INNER, 4 * HEADS), INNER ** -0.5, 0.3125),
        "step_bias": jnp.clip(jax.random.uniform(key_list[7], (4 * HEADS,), jnp.float32, -1.0, 1.0), -1.0, 1.0),
        "decay_log": draw_decay_log(jax.random.fold_in(key_list[12], 71), part),
        "skip_gain": jnp.clip(jnp.exp(jax.random.uniform(key_list[9], (4 * HEADS,), jnp.float32, math.log(0.5), math.log(12.0))), 0.5, 12.0),
        "out_gain": jnp.clip(1.0 + 0.18 * jax.random.normal(key_list[10], (INNER,), jnp.float32), 0.1, 1.9),
        "out_weight": centred(key_list[11], (INNER, WIDTH), INNER ** -0.5, 0.3125),
    }


EPSILON = 1e-05

def rms_scale(values, gain):
    mean_square = lax.optimization_barrier(jnp.mean(values * values, axis=-1, keepdims=True))
    return values * lax.rsqrt(mean_square + EPSILON) * gain

def block_local(signal, writer, reader, log_decay, step_sizes, skip_part):
    seq_length, inner_width = signal.shape
    head_count = log_decay.shape[1]
    head_size = inner_width // head_count
    block_count = seq_length // BLOCK
    value_blocks = signal.reshape(block_count, BLOCK, head_count, head_size)
    writer_blocks = writer.reshape(block_count, BLOCK, -1)
    reader_blocks = reader.reshape(block_count, BLOCK, -1)
    step_blocks = step_sizes.reshape(block_count, BLOCK, head_count)
    cumul = jnp.cumsum(log_decay.reshape(block_count, BLOCK, head_count), axis=1)
    causal = lax.broadcasted_iota(jnp.int32, (BLOCK, BLOCK), 0) >= lax.broadcasted_iota(jnp.int32, (BLOCK, BLOCK), 1)

    def one_block(pieces):
        value_part, writer_part, reader_part, cumul_part, step_part = pieces
        scores = jnp.dot(reader_part, writer_part.T, preferred_element_type=jnp.float32)
        cum_heads = cumul_part.T
        spread = jnp.where(causal[None], cum_heads[:, :, None] - cum_heads[:, None, :], -jnp.inf)
        mixing = (scores[None] * jnp.exp(spread) * step_part.T[:, None, :]).astype(jnp.bfloat16)
        inside = jnp.einsum('hts,shp->thp', mixing.astype(jnp.float32), value_part.astype(jnp.float32))
        tail_weight = jnp.exp(cumul_part[-1][None, :] - cumul_part) * step_part
        weighted = (value_part * tail_weight[:, :, None]).astype(jnp.bfloat16)
        contrib = jnp.einsum('shp,sn->hpn', weighted.astype(jnp.float32), writer_part.astype(jnp.float32))
        return (inside, contrib)
    inside, contrib = lax.map(one_block, (value_blocks, writer_blocks, reader_blocks, cumul, step_blocks))
    decays = cumul[:, -1, :]

    def advance(carried, pieces):
        decay_now, added = pieces
        return (jnp.exp(decay_now)[:, None, None] * carried + added, carried)
    zero_state = jnp.zeros(contrib.shape[1:], jnp.float32)
    closing, starts = lax.scan(advance, zero_state, (decays, contrib))
    before = jnp.cumsum(decays, axis=0) - decays
    own_part = inside + value_blocks.astype(jnp.float32) * skip_part[None, None, :, None]
    return (own_part, starts, before, cumul, reader_blocks)

def finish(local_terms, carried_in):
    own_part, starts, before, cumul, reader_blocks = local_terms
    entry_state = starts + jnp.exp(before)[:, :, None, None] * carried_in[None]
    entry_half = entry_state.astype(jnp.bfloat16)
    outer_part = jnp.einsum('ktn,khpn->kthp', reader_blocks.astype(jnp.float32), entry_half.astype(jnp.float32))
    result = own_part + outer_part * jnp.exp(cumul)[:, :, :, None]
    return result.reshape(-1, result.shape[2] * result.shape[3])

def column_major(values):
    return jnp.transpose(values, (1, 0, 2)).reshape(values.shape[0] * values.shape[1], values.shape[2])

def reference(region, norm_gain, in_weight, conv_weight, conv_bias, coupling_weight, step_weight, step_bias, decay_log, skip_gain, out_gain, out_weight):
    row_count, col_count, feat_width = region.shape
    inner_width = in_weight.shape[1] // 2
    head_count = step_bias.shape[0] // 4
    head_size = inner_width // head_count
    state_size = coupling_weight.shape[1] // 8
    token_count = row_count * col_count
    flat_region = region.reshape(token_count, feat_width).astype(jnp.float32)
    normed = rms_scale(flat_region, norm_gain).astype(jnp.bfloat16)
    projected = jnp.dot(normed, in_weight, preferred_element_type=jnp.float32).astype(jnp.bfloat16)
    pre_conv = projected[:, :inner_width].reshape(row_count, col_count, inner_width)
    gate_part = projected[:, inner_width:]
    padded = jnp.pad(pre_conv, ((1, 1), (1, 1), (0, 0)))
    summed = conv_bias
    for offset_row in range(3):
        for offset_col in range(3):
            summed = summed + padded[offset_row:offset_row + row_count, offset_col:offset_col + col_count] * conv_weight[offset_row * 3 + offset_col]
    activated = jax.nn.silu(summed).astype(jnp.bfloat16)
    flat_active = activated.reshape(token_count, inner_width)
    coupling = jnp.dot(flat_active, coupling_weight, preferred_element_type=jnp.float32).astype(jnp.bfloat16)
    step_sizes = jax.nn.softplus(jnp.dot(flat_active, step_weight, preferred_element_type=jnp.float32) + step_bias)
    log_decay = -jnp.exp(decay_log) * step_sizes
    outputs = []
    for index in range(4):
        pieces = [flat_active, coupling[:, 2 * index * state_size:(2 * index + 1) * state_size], coupling[:, (2 * index + 1) * state_size:(2 * index + 2) * state_size], log_decay[:, index * head_count:(index + 1) * head_count], step_sizes[:, index * head_count:(index + 1) * head_count]]
        if index >= 2:
            pieces = [column_major(piece.reshape(row_count, col_count, -1)) for piece in pieces]
        if index % 2 == 1:
            pieces = [jnp.flip(piece, 0) for piece in pieces]
        local_terms = block_local(pieces[0], pieces[1], pieces[2], pieces[3], pieces[4], skip_gain[index * head_count:(index + 1) * head_count])
        zero_carry = jnp.zeros((head_count, head_size, state_size), jnp.float32)
        order_out = finish(local_terms, zero_carry)
        if index % 2 == 1:
            order_out = jnp.flip(order_out, 0)
        outputs.append(order_out)
    col_total = (outputs[2] + outputs[3]).astype(jnp.bfloat16)
    col_total = jnp.transpose(col_total.reshape(col_count, row_count, inner_width), (1, 0, 2)).reshape(token_count, inner_width)
    combined = outputs[0] + outputs[1] + col_total.astype(jnp.float32)
    gated = combined * jax.nn.silu(gate_part.astype(jnp.float32))
    normy = rms_scale(gated, out_gain).astype(jnp.bfloat16)
    refined = flat_region + jnp.dot(normy, out_weight, preferred_element_type=jnp.float32)
    return refined.astype(jnp.bfloat16).reshape(row_count, col_count, feat_width)
```

```python
import functools
import jax
import jax.numpy as jnp
from jax import lax
from jax.experimental import pallas as pl
from jax.experimental.pallas import tpu as pltpu
from jax.sharding import PartitionSpec as P

EPSILON = 1e-05
BF = jnp.bfloat16
F32 = jnp.float32
TILE = 128


def mm(a, b):
    return jnp.dot(a, b, preferred_element_type=F32)


def mm_nt(a, b):
    return lax.dot_general(a, b, (((1,), (1,)), ((), ())), preferred_element_type=F32)


def mm_tn(a, b):
    return lax.dot_general(a, b, (((0,), (0,)), ((), ())), preferred_element_type=F32)


def split3(v):
    hi = v.astype(BF)
    rest = v - hi.astype(F32)
    mid = rest.astype(BF)
    lo = (rest - mid.astype(F32)).astype(BF)
    return hi, mid, lo


def iota(shape, dim):
    return lax.broadcasted_iota(jnp.int32, shape, dim)


def kernel(
    n,
    heads,
    state,
    region_ref,
    norm_gain_ref,
    in_w_ref,
    conv_w_ref,
    conv_b_ref,
    coup_w_ref,
    step_w_ref,
    step_b_ref,
    decay_ref,
    skip_ref,
    out_gain_ref,
    out_w_ref,
    out_ref,
    halo,
    pre,
    gate,
    act,
    colbuf,
    xcol,
    xe,
    xo,
    coup,
    cum,
    cum_t,
    step_t,
    own_row,
    own_col,
    msg,
    got,
    ent_out,
    ent_in,
    col_out,
    col_in,
    halo_send,
    halo_recv,
    a_send,
    a_recv,
    s_send,
    s_recv,
    e_send,
    e_recv,
    c_send,
    c_recv,
):
    me = lax.axis_index("seq")
    tokens, width = region_ref.shape[1], region_ref.shape[2]
    inner = out_w_ref.shape[0]
    band = tokens // n
    head = inner // heads
    part = state // n
    head_bits = head.bit_length() - 1
    n_bits = n.bit_length() - 1
    band_bits = band.bit_length() - 1
    groups = 4 * heads

    def peer_of(k):
        return lax.rem(me + k, n)

    def source_of(k):
        return lax.rem(me + n - k, n)

    barrier = pltpu.get_barrier_semaphore()

    def greet(k, _):
        pl.semaphore_signal(barrier, inc=1, device_id={"seq": peer_of(k)})
        return 0

    lax.fori_loop(1, n, greet, 0)
    pl.semaphore_wait(barrier, n - 1)

    def halo_copy(slot, device):
        return pltpu.make_async_remote_copy(
            src_ref=region_ref.at[0],
            dst_ref=halo.at[slot],
            send_sem=halo_send.at[slot],
            recv_sem=halo_recv.at[slot],
            device_id={"seq": device},
        )

    @pl.when(me < n - 1)
    def _():
        halo_copy(0, me + 1).start()

    @pl.when(me > 0)
    def _():
        halo_copy(1, me - 1).start()

    def normed(values):
        mean_square = jnp.mean(values * values, axis=-1, keepdims=True)
        return (values * lax.rsqrt(mean_square + EPSILON) * norm_gain_ref[...]).astype(BF)

    edge = jnp.zeros((8, inner), F32)
    for a in range(3):
        pre[a, 0:8, :] = edge
        pre[a, tokens + 8 : tokens + 16, :] = edge
    own = mm(normed(region_ref[0].astype(F32)), in_w_ref[...]).astype(BF)
    pre[1, 8 : tokens + 8, :] = own[:, :inner].astype(F32)
    gate[...] = own[:, inner:]

    @pl.when(me < n - 1)
    def _():
        halo_copy(1, me + 1).wait_recv()
        halo_copy(0, me + 1).wait_send()

    @pl.when(me == n - 1)
    def _():
        halo[1] = jnp.zeros((tokens, width), BF)

    @pl.when(me > 0)
    def _():
        halo_copy(0, me - 1).wait_recv()
        halo_copy(1, me - 1).wait_send()

    @pl.when(me == 0)
    def _():
        halo[0] = jnp.zeros((tokens, width), BF)

    for slot, a in ((0, 0), (1, 2)):
        rim = mm(normed(halo[slot].astype(F32)), in_w_ref[:, :inner]).astype(BF)
        pre[a, 8 : tokens + 8, :] = rim.astype(F32)

    per = TILE // band if band < TILE else 1
    for c in range(tokens // TILE):
        summed = conv_b_ref[...]
        for a in range(3):
            for b in range(3):
                first = c * TILE + 7 + b
                tap = 3 * a + b
                summed = summed + pre[a, first : first + TILE, :] * conv_w_ref[tap : tap + 1, :]
        done = (summed / (1.0 + jnp.exp(-summed))).astype(BF)
        if band <= TILE:
            act[c * per : (c + 1) * per] = done.reshape(per, band, inner)
        else:
            where = c * TILE // band
            start = c * TILE % band
            act[where, start : start + TILE] = done

    def a_copy(k, chunk, place):
        return pltpu.make_async_remote_copy(
            src_ref=act.at[chunk],
            dst_ref=colbuf.at[place],
            send_sem=a_send.at[k],
            recv_sem=a_recv.at[k],
            device_id={"seq": chunk},
        )

    def s_copy(p, k, chunk, place):
        return pltpu.make_async_remote_copy(
            src_ref=msg.at[p, chunk],
            dst_ref=got.at[p, place],
            send_sem=s_send.at[p, k],
            recv_sem=s_recv.at[p, k],
            device_id={"seq": chunk},
        )

    def e_copy(p, k, chunk, place):
        return pltpu.make_async_remote_copy(
            src_ref=ent_out.at[p, chunk],
            dst_ref=ent_in.at[p, place],
            send_sem=e_send.at[p, k],
            recv_sem=e_recv.at[p, k],
            device_id={"seq": chunk},
        )

    def c_copy(k, chunk, place):
        return pltpu.make_async_remote_copy(
            src_ref=col_out.at[chunk],
            dst_ref=col_in.at[place],
            send_sem=c_send.at[k],
            recv_sem=c_recv.at[k],
            device_id={"seq": chunk},
        )

    def start_all(make):
        def one(k, _):
            make(k, peer_of(k), me).start()
            return 0

        lax.fori_loop(1, n, one, 0)

    def wait_all(make):
        def one(k, _):
            make(k, peer_of(k), source_of(k)).wait_recv()
            return 0

        lax.fori_loop(1, n, one, 0)

    def wait_sent(make):
        def one(k, _):
            make(k, peer_of(k), source_of(k)).wait_send()
            return 0

        lax.fori_loop(1, n, one, 0)

    start_all(a_copy)
    colbuf[pl.ds(me, 1)] = act[pl.ds(me, 1)]

    group_lane = iota((1, groups), 1)
    behind_lane = lax.rem(group_lane, 2 * heads) >= heads
    lower = (iota((tokens, tokens), 0) >= iota((tokens, tokens), 1)).astype(BF)
    eye = (iota((groups, groups), 0) == iota((groups, groups), 1)).astype(BF)
    spread_row = iota((groups, inner), 0)
    spread_head = jnp.right_shift(iota((groups, inner), 1), head_bits)
    rates = -jnp.exp(decay_ref[...])

    def spreader(base):
        return (spread_row == base + spread_head).astype(BF)

    def expand(v, e):
        hi, mid, lo = split3(v)
        return mm(hi, e) + mm(mid, e) + mm(lo, e)

    def flip_axes(v):
        hi, mid, lo = split3(v)
        return mm_nt(eye, hi) + mm_nt(eye, mid) + mm_nt(eye, lo)

    def prepare(p, x):
        first = p * 4 * state
        coup[p] = mm(x, coup_w_ref[:, first : first + 4 * state]).astype(BF)
        logits = mm(x, step_w_ref[...]) + step_b_ref[...]
        steps = jnp.maximum(logits, 0.0) + jnp.log1p(jnp.exp(-jnp.abs(logits)))
        logs = rates * steps
        hi, mid, lo = split3(logs)
        ahead = mm(lower, hi) + mm(lower, mid) + mm(lower, lo)
        total = ahead[tokens - 1 : tokens, :]
        c = jnp.where(behind_lane, total - ahead + logs, ahead)
        cum[p] = c
        cum_t[p] = flip_axes(c)
        step_t[p] = flip_axes(steps)
        tail = jnp.exp(total - c) * steps
        base = p * 2 * heads
        xf = x.astype(F32)
        spread_a, spread_b = spreader(base), spreader(base + heads)
        totals = jnp.broadcast_to(total, (8, groups))
        for o, e in ((0, spread_a), (1, spread_b)):
            weighted = (xf * expand(tail, e)).astype(BF)
            writer = coup[p, :, 2 * o * state : (2 * o + 1) * state]
            contrib = mm_tn(writer, weighted)
            decay = expand(totals, e)[0:1]
            for d in range(n):
                msg[p, d, o * part : (o + 1) * part, :] = contrib[d * part : (d + 1) * part]
                msg[p, d, 2 * part + o : 2 * part + o + 1, :] = decay
        start_all(functools.partial(s_copy, p))
        got[p, pl.ds(me, 1)] = msg[p, pl.ds(me, 1)]
        def diagonal(o):
            w = coup[p, :, 2 * o * state : (2 * o + 1) * state].astype(F32)
            r = coup[p, :, (2 * o + 1) * state : (2 * o + 2) * state].astype(F32)
            return jnp.sum(w * r, axis=-1, keepdims=True)

        diag = (jnp.where(behind_lane, diagonal(1), diagonal(0)) * steps).astype(BF).astype(F32)
        target = own_col if p else own_row
        target[...] = xf * expand(diag + skip_ref[...], spread_a + spread_b)
        even = jnp.bitwise_and(iota((1, inner), 1), head) == 0
        xe[...] = jnp.where(even, xf, 0.0).astype(BF)
        xo[...] = jnp.where(even, 0.0, xf).astype(BF)

    def mix(p):
        target = own_col if p else own_row

        def tile(i, _):
            t0 = pl.multiple_of(i * TILE, TILE)
            rows = pl.ds(t0, TILE)
            both = coup[p, rows, :]
            ahead = mm_nt(both[:, state : 2 * state], coup[p, :, 0:state])
            behind = mm_nt(both[:, 3 * state : 4 * state], coup[p, :, 2 * state : 3 * state])
            t = iota((TILE, tokens), 0) + t0
            s = iota((TILE, tokens), 1)
            after = t > s
            scores = jnp.where(after, ahead, jnp.where(t < s, behind, 0.0))
            c = cum[p, rows, :]

            def weights(h):
                f = p * 2 * heads + h
                g = f + heads
                lead = c[:, f : f + 1] - cum_t[p, f : f + 1, :]
                back = c[:, g : g + 1] - cum_t[p, g : g + 1, :]
                step = jnp.where(after, step_t[p, f : f + 1, :], step_t[p, g : g + 1, :])
                return (scores * jnp.exp(jnp.minimum(lead, back)) * step).astype(BF)

            for j in range(heads // 2):
                lanes = slice(2 * j * head, 2 * (j + 1) * head)
                inside = mm(weights(2 * j), xe[:, lanes]) + mm(weights(2 * j + 1), xo[:, lanes])
                target[rows, lanes] += inside
            return 0

        lax.fori_loop(0, tokens // TILE, tile, 0)

    def scan(p):
        wait_all(functools.partial(s_copy, p))
        entry = jnp.zeros((part, inner), F32)
        ahead = []
        for i in range(n):
            ahead.append(entry)
            decay = jnp.exp(got[p, i, 2 * part : 2 * part + 1, :])
            entry = decay * entry + got[p, i, 0:part, :]
        entry = jnp.zeros((part, inner), F32)
        for i in reversed(range(n)):
            pieces = [ahead[i], entry]
            if 2 * part < 16:
                pieces.append(jnp.zeros((16 - 2 * part, inner), F32))
            ent_out[p, i] = jnp.concatenate(pieces, axis=0).astype(BF)
            decay = jnp.exp(got[p, i, 2 * part + 1 : 2 * part + 2, :])
            entry = decay * entry + got[p, i, part : 2 * part, :]
        start_all(functools.partial(e_copy, p))
        ent_in[p, pl.ds(me, 1)] = ent_out[p, pl.ds(me, 1)]

    def finish(p):
        wait_all(functools.partial(e_copy, p))
        target = own_col if p else own_row
        arrived = [ent_in[p, i].astype(F32) for i in range(n)]
        grown = jnp.exp(cum[p])
        base = p * 2 * heads
        result = target[...]
        for o in range(2):
            entry = jnp.concatenate(
                [v[o * part : (o + 1) * part] for v in arrived], axis=0
            ).astype(BF)
            reader = coup[p, :, (2 * o + 1) * state : (2 * o + 2) * state]
            result = result + mm(reader, entry) * expand(grown, spreader(base + o * heads))
        return result

    x_row = act[...].reshape(tokens, inner)
    prepare(0, x_row)
    mix(0)
    wait_all(a_copy)
    place = iota((tokens, tokens), 0)
    cell = iota((tokens, tokens), 1)
    turn = cell == jnp.left_shift(jnp.bitwise_and(place, n - 1), band_bits) + jnp.right_shift(place, n_bits)
    xcol[...] = mm(turn.astype(BF), colbuf[...].reshape(tokens, inner)).astype(BF)
    prepare(1, xcol[...])
    scan(0)
    mix(1)
    scan(1)
    column = finish(1).astype(BF)
    back = cell == jnp.left_shift(jnp.bitwise_and(place, band - 1), n_bits) + jnp.right_shift(place, band_bits)
    col_out[...] = mm(back.astype(BF), column).astype(BF).reshape(n, band, inner)
    start_all(c_copy)
    col_in[pl.ds(me, 1)] = col_out[pl.ds(me, 1)]
    row_total = finish(0)
    g = gate[...].astype(F32)
    own_row[...] = row_total
    own_col[...] = g / (1.0 + jnp.exp(-g))
    wait_all(c_copy)
    for c in range(tokens // TILE):
        rows = slice(c * TILE, (c + 1) * TILE)
        if band <= TILE:
            col = col_in[c * per : (c + 1) * per].reshape(TILE, inner)
        else:
            start = c * TILE % band
            col = col_in[c * TILE // band, start : start + TILE]
        gated = (own_row[rows, :] + col.astype(F32)) * own_col[rows, :]
        mean_square = jnp.mean(gated * gated, axis=-1, keepdims=True)
        normy = (gated * lax.rsqrt(mean_square + EPSILON) * out_gain_ref[...]).astype(BF)
        out_ref[0, rows, :] = (
            region_ref[0, rows, :].astype(F32) + mm(normy, out_w_ref[...])
        ).astype(BF)
    wait_sent(a_copy)
    for p in range(2):
        wait_sent(functools.partial(s_copy, p))
        wait_sent(functools.partial(e_copy, p))
    wait_sent(c_copy)


def body(n, *args):
    region = args[0]
    rows, tokens, width = region.shape
    inner = args[11].shape[0]
    groups = args[7].shape[0]
    heads = groups // 4
    state = args[5].shape[1] // 8
    band = tokens // n
    part = state // n
    flat = [v if v.ndim > 1 else v.reshape(1, -1) for v in args]
    msg_rows = 2 * part + 2
    ent_rows = max(16, 2 * part)
    dma = pltpu.SemaphoreType.DMA
    vmem = pltpu.VMEM
    return pl.pallas_call(
        functools.partial(kernel, n, heads, state),
        out_shape=jax.ShapeDtypeStruct(region.shape, BF),
        in_specs=[pl.BlockSpec(memory_space=pltpu.VMEM)] * len(flat),
        out_specs=pl.BlockSpec(memory_space=pltpu.VMEM),
        scratch_shapes=[
            vmem((2, tokens, width), BF),
            vmem((3, tokens + 16, inner), F32),
            vmem((tokens, inner), BF),
            vmem((n, band, inner), BF),
            vmem((n, band, inner), BF),
            vmem((tokens, inner), BF),
            vmem((tokens, inner), BF),
            vmem((tokens, inner), BF),
            vmem((2, tokens, 4 * state), BF),
            vmem((2, tokens, groups), F32),
            vmem((2, groups, tokens), F32),
            vmem((2, groups, tokens), F32),
            vmem((tokens, inner), F32),
            vmem((tokens, inner), F32),
            vmem((2, n, msg_rows, inner), F32),
            vmem((2, n, msg_rows, inner), F32),
            vmem((2, n, ent_rows, inner), BF),
            vmem((2, n, ent_rows, inner), BF),
            vmem((n, band, inner), BF),
            vmem((n, band, inner), BF),
            dma((2,)),
            dma((2,)),
            dma((n,)),
            dma((n,)),
            dma((2, n)),
            dma((2, n)),
            dma((2, n)),
            dma((2, n)),
            dma((n,)),
            dma((n,)),
        ],
        compiler_params=pltpu.CompilerParams(
            collective_id=0, has_side_effects=True, vmem_limit_bytes=50 * 1024 * 1024
        ),
    )(*flat)


def solution(mesh):
    in_specs = (P(("dp", "seq"), None, None),) + (P(),) * 11
    return jax.shard_map(
        functools.partial(body, mesh.shape["seq"]),
        mesh=mesh,
        in_specs=in_specs,
        out_specs=P(("dp", "seq"), None, None),
        check_vma=False,
    )
```

```python
import functools
import jax
import jax.numpy as jnp
from jax import lax
from jax.experimental import pallas as pl
from jax.experimental.pallas import tpu as pltpu
from jax.sharding import PartitionSpec as P

EPSILON = 1e-05
BF = jnp.bfloat16
F32 = jnp.float32
TILE = 128


def mm(a, b):
    return jnp.dot(a, b, preferred_element_type=F32)


def mm_nt(a, b):
    return lax.dot_general(a, b, (((1,), (1,)), ((), ())), preferred_element_type=F32)


def mm_tn(a, b):
    return lax.dot_general(a, b, (((0,), (0,)), ((), ())), preferred_element_type=F32)


def split3(v):
    hi = v.astype(BF)
    rest = v - hi.astype(F32)
    mid = rest.astype(BF)
    lo = (rest - mid.astype(F32)).astype(BF)
    return hi, mid, lo


def iota(shape, dim):
    return lax.broadcasted_iota(jnp.int32, shape, dim)


def kernel(
    n,
    heads,
    state,
    region_ref,
    norm_gain_ref,
    in_w_ref,
    conv_w_ref,
    conv_b_ref,
    coup_w_ref,
    step_w_ref,
    step_b_ref,
    decay_ref,
    skip_ref,
    out_gain_ref,
    out_w_ref,
    out_ref,
    halo,
    pre,
    gate,
    act,
    colbuf,
    xcol,
    xe,
    xo,
    coup,
    cum,
    cum_t,
    step_t,
    own_row,
    own_col,
    msg,
    got,
    tot,
    got_tot,
    ent_out,
    ent_in,
    col_out,
    col_in,
    halo_send,
    halo_recv,
    a_send,
    a_recv,
    s_send,
    s_recv,
    t_send,
    t_recv,
    e_send,
    e_recv,
    c_send,
    c_recv,
):
    me = lax.axis_index("seq")
    tokens, width = region_ref.shape[1], region_ref.shape[2]
    inner = out_w_ref.shape[1]
    band = tokens // n
    head = inner // heads
    part = state // n
    head_bits = head.bit_length() - 1
    n_bits = n.bit_length() - 1
    band_bits = band.bit_length() - 1
    groups = 4 * heads

    def peer_of(k):
        return lax.rem(me + k, n)

    def source_of(k):
        return lax.rem(me + n - k, n)

    barrier = pltpu.get_barrier_semaphore()

    def greet(k, _):
        pl.semaphore_signal(barrier, inc=1, device_id={"seq": peer_of(k)})
        return 0

    lax.fori_loop(1, n, greet, 0)
    pl.semaphore_wait(barrier, n - 1)

    def halo_copy(slot, device):
        return pltpu.make_async_remote_copy(
            src_ref=region_ref.at[0],
            dst_ref=halo.at[slot],
            send_sem=halo_send.at[slot],
            recv_sem=halo_recv.at[slot],
            device_id={"seq": device},
        )

    @pl.when(me < n - 1)
    def _():
        halo_copy(0, me + 1).start()

    @pl.when(me > 0)
    def _():
        halo_copy(1, me - 1).start()

    def normed(values):
        mean_square = jnp.mean(values * values, axis=-1, keepdims=True)
        return (values * lax.rsqrt(mean_square + EPSILON) * norm_gain_ref[...]).astype(BF)

    edge = jnp.zeros((8, inner), F32)
    for a in range(3):
        pre[a, 0:8, :] = edge
        pre[a, tokens + 8 : tokens + 16, :] = edge
    own = mm(normed(region_ref[0].astype(F32)), in_w_ref[...]).astype(BF)
    pre[1, 8 : tokens + 8, :] = own[:, :inner].astype(F32)
    gate[...] = own[:, inner:]

    @pl.when(me < n - 1)
    def _():
        halo_copy(1, me + 1).wait_recv()
        halo_copy(0, me + 1).wait_send()

    @pl.when(me == n - 1)
    def _():
        halo[1] = jnp.zeros((tokens, width), BF)

    @pl.when(me > 0)
    def _():
        halo_copy(0, me - 1).wait_recv()
        halo_copy(1, me - 1).wait_send()

    @pl.when(me == 0)
    def _():
        halo[0] = jnp.zeros((tokens, width), BF)

    for slot, a in ((0, 0), (1, 2)):
        rim = mm(normed(halo[slot].astype(F32)), in_w_ref[:, :inner]).astype(BF)
        pre[a, 8 : tokens + 8, :] = rim.astype(F32)

    per = TILE // band if band < TILE else 1
    for c in range(tokens // TILE):
        summed = conv_b_ref[...]
        for a in range(3):
            for b in range(3):
                first = c * TILE + 7 + b
                tap = 3 * a + b
                summed = summed + pre[a, first : first + TILE, :] * conv_w_ref[tap : tap + 1, :]
        done = (summed / (1.0 + jnp.exp(-summed))).astype(BF)
        if band <= TILE:
            act[c * per : (c + 1) * per] = done.reshape(per, band, inner)
        else:
            where = c * TILE // band
            start = c * TILE % band
            act[where, start : start + TILE] = done

    def a_copy(k, chunk, place):
        return pltpu.make_async_remote_copy(
            src_ref=act.at[chunk],
            dst_ref=colbuf.at[place],
            send_sem=a_send.at[k],
            recv_sem=a_recv.at[k],
            device_id={"seq": chunk},
        )

    def s_copy(p, k, chunk, place):
        return pltpu.make_async_remote_copy(
            src_ref=msg.at[p, chunk],
            dst_ref=got.at[p, place],
            send_sem=s_send.at[p, k],
            recv_sem=s_recv.at[p, k],
            device_id={"seq": chunk},
        )

    def t_copy(p, k, chunk, place):
        return pltpu.make_async_remote_copy(
            src_ref=tot.at[p],
            dst_ref=got_tot.at[p, place],
            send_sem=t_send.at[p, k],
            recv_sem=t_recv.at[p, k],
            device_id={"seq": chunk},
        )

    def e_copy(p, k, chunk, place):
        return pltpu.make_async_remote_copy(
            src_ref=ent_out.at[p, chunk],
            dst_ref=ent_in.at[p, place],
            send_sem=e_send.at[p, k],
            recv_sem=e_recv.at[p, k],
            device_id={"seq": chunk},
        )

    def c_copy(k, chunk, place):
        return pltpu.make_async_remote_copy(
            src_ref=col_out.at[chunk],
            dst_ref=col_in.at[place],
            send_sem=c_send.at[k],
            recv_sem=c_recv.at[k],
            device_id={"seq": chunk},
        )

    def start_all(make):
        def one(k, _):
            make(k, peer_of(k), me).start()
            return 0

        lax.fori_loop(1, n, one, 0)

    def wait_all(make):
        def one(k, _):
            make(k, peer_of(k), source_of(k)).wait_recv()
            return 0

        lax.fori_loop(1, n, one, 0)

    def wait_sent(make):
        def one(k, _):
            make(k, peer_of(k), source_of(k)).wait_send()
            return 0

        lax.fori_loop(1, n, one, 0)

    start_all(a_copy)
    colbuf[pl.ds(me, 1)] = act[pl.ds(me, 1)]

    group_lane = iota((1, groups), 1)
    behind_lane = lax.rem(group_lane, 2 * heads) >= heads
    lower = (iota((tokens, tokens), 0) >= iota((tokens, tokens), 1)).astype(BF)
    eye = (iota((groups, groups), 0) == iota((groups, groups), 1)).astype(BF)
    spread_row = iota((groups, inner), 0)
    spread_head = jnp.right_shift(iota((groups, inner), 1), head_bits)
    rates = -jnp.exp(decay_ref[...])

    def spreader(base):
        return (spread_row == base + spread_head).astype(F32)

    def expand(v, e):
        hi, mid, lo = (piece.astype(F32) for piece in split3(v))
        pieces = jnp.concatenate([hi, mid, lo], axis=1).astype(BF)
        return mm(pieces, jnp.concatenate([e, e, e], axis=0).astype(BF))

    def flip_axes(v):
        hi, mid, lo = split3(v)
        return mm_nt(eye, hi) + mm_nt(eye, mid) + mm_nt(eye, lo)

    def prepare(p, x):
        first = p * 4 * state
        coup[p] = mm(x, coup_w_ref[:, first : first + 4 * state]).astype(BF)
        logits = mm_nt(x, step_w_ref[...]) + step_b_ref[...]
        steps = jnp.maximum(logits, 0.0) + jnp.log1p(jnp.exp(-jnp.abs(logits)))
        logs = rates * steps
        hi, mid, lo = split3(logs)
        ahead = mm(lower, hi) + mm(lower, mid) + mm(lower, lo)
        total = ahead[tokens - 1 : tokens, :]
        c = jnp.where(behind_lane, total - ahead + logs, ahead)
        cum[p] = c
        cum_t[p] = flip_axes(c)
        step_t[p] = flip_axes(steps)
        tail = jnp.exp(total - c) * steps
        base = p * 2 * heads
        xf = x.astype(F32)
        spread_a, spread_b = spreader(base), spreader(base + heads)
        tot[p, :, 0:groups] = jnp.broadcast_to(total, (8, groups))
        start_all(functools.partial(t_copy, p))
        got_tot[p, pl.ds(me, 1)] = tot[p][None]
        contribs = []
        for o, e in ((0, spread_a), (1, spread_b)):
            weighted = (xf * expand(tail, e)).astype(BF)
            writer = coup[p, :, 2 * o * state : (2 * o + 1) * state]
            contribs.append(mm_tn(writer, weighted))
        for d in range(n):
            pieces = [v[d * part : (d + 1) * part] for v in contribs]
            if 2 * part < 16:
                pieces.append(jnp.zeros((16 - 2 * part, inner), F32))
            msg[p, d] = jnp.concatenate(pieces, axis=0).astype(BF)
        start_all(functools.partial(s_copy, p))
        got[p, pl.ds(me, 1)] = msg[p, pl.ds(me, 1)]
        def diagonal(o):
            w = coup[p, :, 2 * o * state : (2 * o + 1) * state].astype(F32)
            r = coup[p, :, (2 * o + 1) * state : (2 * o + 2) * state].astype(F32)
            return jnp.sum(w * r, axis=-1, keepdims=True)

        diag = (jnp.where(behind_lane, diagonal(1), diagonal(0)) * steps).astype(BF).astype(F32)
        target = own_col if p else own_row
        target[...] = xf * expand(diag + skip_ref[...], spread_a + spread_b)
        even = jnp.bitwise_and(iota((1, inner), 1), head) == 0
        xe[...] = jnp.where(even, xf, 0.0).astype(BF)
        xo[...] = jnp.where(even, 0.0, xf).astype(BF)

    def mix(p, first, last):
        target = own_col if p else own_row

        def tile(i, _):
            t0 = pl.multiple_of(i * TILE, TILE)
            rows = pl.ds(t0, TILE)
            both = coup[p, rows, :]
            ahead = mm_nt(both[:, state : 2 * state], coup[p, :, 0:state])
            behind = mm_nt(both[:, 3 * state : 4 * state], coup[p, :, 2 * state : 3 * state])
            t = iota((TILE, tokens), 0) + t0
            s = iota((TILE, tokens), 1)
            after = t > s
            scores = jnp.where(after, ahead, jnp.where(t < s, behind, 0.0))
            c = cum[p, rows, :]

            def weights(h):
                f = p * 2 * heads + h
                g = f + heads
                lead = c[:, f : f + 1] - cum_t[p, f : f + 1, :]
                back = c[:, g : g + 1] - cum_t[p, g : g + 1, :]
                step = jnp.where(after, step_t[p, f : f + 1, :], step_t[p, g : g + 1, :])
                return (scores * jnp.exp(jnp.minimum(lead, back)) * step).astype(BF)

            for j in range(heads // 2):
                lanes = slice(2 * j * head, 2 * (j + 1) * head)
                inside = mm(weights(2 * j), xe[:, lanes]) + mm(weights(2 * j + 1), xo[:, lanes])
                target[rows, lanes] += inside
            return 0

        lax.fori_loop(first, last, tile, 0)

    def scan(p):
        wait_all(functools.partial(t_copy, p))
        base = p * 2 * heads
        totals = jnp.exp(
            jnp.concatenate([got_tot[p, i, 0:8, 0:groups] for i in range(n)], axis=0)
        )
        fade_a = expand(totals, spreader(base))
        fade_b = expand(totals, spreader(base + heads))
        wait_all(functools.partial(s_copy, p))
        entry = jnp.zeros((part, inner), F32)
        ahead = []
        for i in range(n):
            ahead.append(entry)
            entry = fade_a[8 * i : 8 * i + 1] * entry + got[p, i].astype(F32)[0:part]
        entry = jnp.zeros((part, inner), F32)
        for i in reversed(range(n)):
            pieces = [ahead[i], entry]
            if 2 * part < 16:
                pieces.append(jnp.zeros((16 - 2 * part, inner), F32))
            ent_out[p, i] = jnp.concatenate(pieces, axis=0).astype(BF)
            entry = fade_b[8 * i : 8 * i + 1] * entry + got[p, i].astype(F32)[part : 2 * part]
        start_all(functools.partial(e_copy, p))
        ent_in[p, pl.ds(me, 1)] = ent_out[p, pl.ds(me, 1)]

    def finish(p):
        wait_all(functools.partial(e_copy, p))
        target = own_col if p else own_row
        arrived = [ent_in[p, i].astype(F32) for i in range(n)]
        grown = jnp.exp(cum[p])
        base = p * 2 * heads
        result = target[...]
        for o in range(2):
            entry = jnp.concatenate(
                [v[o * part : (o + 1) * part] for v in arrived], axis=0
            ).astype(BF)
            reader = coup[p, :, (2 * o + 1) * state : (2 * o + 2) * state]
            result = result + mm(reader, entry) * expand(grown, spreader(base + o * heads))
        return result

    x_row = act[...].reshape(tokens, inner)
    prepare(0, x_row)
    tiles = tokens // TILE
    mix(0, 0, tiles)
    wait_all(a_copy)
    place = iota((tokens, tokens), 0)
    cell = iota((tokens, tokens), 1)
    turn = cell == jnp.left_shift(jnp.bitwise_and(place, n - 1), band_bits) + jnp.right_shift(place, n_bits)
    xcol[...] = mm(turn.astype(BF), colbuf[...].reshape(tokens, inner)).astype(BF)
    prepare(1, xcol[...])
    scan(0)
    mix(1, 0, tiles // 2)
    scan(1)
    mix(1, tiles // 2, tiles)
    column = finish(1).astype(BF)
    back = cell == jnp.left_shift(jnp.bitwise_and(place, band - 1), n_bits) + jnp.right_shift(place, band_bits)
    col_out[...] = mm(back.astype(BF), column).astype(BF).reshape(n, band, inner)
    start_all(c_copy)
    col_in[pl.ds(me, 1)] = col_out[pl.ds(me, 1)]
    row_total = finish(0)
    g = gate[...].astype(F32)
    own_row[...] = row_total
    own_col[...] = g / (1.0 + jnp.exp(-g))
    wait_all(c_copy)
    for c in range(tokens // TILE):
        rows = slice(c * TILE, (c + 1) * TILE)
        if band <= TILE:
            col = col_in[c * per : (c + 1) * per].reshape(TILE, inner)
        else:
            start = c * TILE % band
            col = col_in[c * TILE // band, start : start + TILE]
        gated = (own_row[rows, :] + col.astype(F32)) * own_col[rows, :]
        mean_square = jnp.mean(gated * gated, axis=-1, keepdims=True)
        normy = (gated * lax.rsqrt(mean_square + EPSILON) * out_gain_ref[...]).astype(BF)
        out_ref[0, rows, :] = (
            region_ref[0, rows, :].astype(F32) + mm_nt(normy, out_w_ref[...])
        ).astype(BF)
    wait_sent(a_copy)
    for p in range(2):
        wait_sent(functools.partial(s_copy, p))
        wait_sent(functools.partial(t_copy, p))
        wait_sent(functools.partial(e_copy, p))
    wait_sent(c_copy)


def body(n, *args):
    region = args[0]
    rows, tokens, width = region.shape
    inner = args[11].shape[0]
    groups = args[7].shape[0]
    heads = groups // 4
    state = args[5].shape[1] // 8
    band = tokens // n
    part = state // n
    flat = [v if v.ndim > 1 else v.reshape(1, -1) for v in args]
    flat[6] = flat[6].T
    flat[11] = flat[11].T
    ent_rows = max(16, 2 * part)
    dma = pltpu.SemaphoreType.DMA
    vmem = pltpu.VMEM
    return pl.pallas_call(
        functools.partial(kernel, n, heads, state),
        out_shape=jax.ShapeDtypeStruct(region.shape, BF),
        in_specs=[pl.BlockSpec(memory_space=pltpu.VMEM)] * len(flat),
        out_specs=pl.BlockSpec(memory_space=pltpu.VMEM),
        scratch_shapes=[
            vmem((2, tokens, width), BF),
            vmem((3, tokens + 16, inner), F32),
            vmem((tokens, inner), BF),
            vmem((n, band, inner), BF),
            vmem((n, band, inner), BF),
            vmem((tokens, inner), BF),
            vmem((tokens, inner), BF),
            vmem((tokens, inner), BF),
            vmem((2, tokens, 4 * state), BF),
            vmem((2, tokens, groups), F32),
            vmem((2, groups, tokens), F32),
            vmem((2, groups, tokens), F32),
            vmem((tokens, inner), F32),
            vmem((tokens, inner), F32),
            vmem((2, n, ent_rows, inner), BF),
            vmem((2, n, ent_rows, inner), BF),
            vmem((2, 8, 128), F32),
            vmem((2, n, 8, 128), F32),
            vmem((2, n, ent_rows, inner), BF),
            vmem((2, n, ent_rows, inner), BF),
            vmem((n, band, inner), BF),
            vmem((n, band, inner), BF),
            dma((2,)),
            dma((2,)),
            dma((n,)),
            dma((n,)),
            dma((2, n)),
            dma((2, n)),
            dma((2, n)),
            dma((2, n)),
            dma((2, n)),
            dma((2, n)),
            dma((n,)),
            dma((n,)),
        ],
        compiler_params=pltpu.CompilerParams(
            collective_id=0, has_side_effects=True, vmem_limit_bytes=50 * 1024 * 1024
        ),
    )(*flat)


def solution(mesh):
    in_specs = (P(("dp", "seq"), None, None),) + (P(),) * 11
    return jax.shard_map(
        functools.partial(body, mesh.shape["seq"]),
        mesh=mesh,
        in_specs=in_specs,
        out_specs=P(("dp", "seq"), None, None),
        check_vma=False,
    )
```

```python
import functools
import jax
import jax.numpy as jnp
from jax import lax
from jax.experimental import pallas as pl
from jax.experimental.pallas import tpu as pltpu
from jax.sharding import PartitionSpec as P

EPSILON = 1e-05
BF = jnp.bfloat16
F32 = jnp.float32
TILE = 128


def mm(a, b):
    return jnp.dot(a, b, preferred_element_type=F32)


def mm_nt(a, b):
    return lax.dot_general(a, b, (((1,), (1,)), ((), ())), preferred_element_type=F32)


def mm_tn(a, b):
    return lax.dot_general(a, b, (((0,), (0,)), ((), ())), preferred_element_type=F32)


def split3(v):
    hi = v.astype(BF)
    rest = v - hi.astype(F32)
    mid = rest.astype(BF)
    lo = (rest - mid.astype(F32)).astype(BF)
    return hi, mid, lo


def iota(shape, dim):
    return lax.broadcasted_iota(jnp.int32, shape, dim)


def kernel(
    n,
    heads,
    state,
    region_ref,
    norm_gain_ref,
    in_w_ref,
    conv_w_ref,
    conv_b_ref,
    coup_w_ref,
    step_w_ref,
    step_b_ref,
    decay_ref,
    skip_ref,
    out_gain_ref,
    out_w_ref,
    out_ref,
    halo,
    pre,
    gate,
    act,
    colbuf,
    xcol,
    xe,
    xo,
    coup,
    cum,
    cum_t,
    step_t,
    own_row,
    own_col,
    msg,
    got,
    tot,
    got_tot,
    ent_out,
    ent_in,
    col_out,
    col_in,
    halo_send,
    halo_recv,
    a_send,
    a_recv,
    s_send,
    s_recv,
    t_send,
    t_recv,
    e_send,
    e_recv,
    c_send,
    c_recv,
):
    me = lax.axis_index("seq")
    width, tokens = region_ref.shape
    inner = out_w_ref.shape[1]
    band = tokens // n
    head = inner // heads
    part = state // n
    head_bits = head.bit_length() - 1
    n_bits = n.bit_length() - 1
    band_bits = band.bit_length() - 1
    groups = 4 * heads

    def peer_of(k):
        return lax.rem(me + k, n)

    def source_of(k):
        return lax.rem(me + n - k, n)

    barrier = pltpu.get_barrier_semaphore()

    def greet(k, _):
        pl.semaphore_signal(barrier, inc=1, device_id={"seq": peer_of(k)})
        return 0

    lax.fori_loop(1, n, greet, 0)
    pl.semaphore_wait(barrier, n - 1)

    def halo_copy(slot, device):
        return pltpu.make_async_remote_copy(
            src_ref=region_ref,
            dst_ref=halo.at[slot],
            send_sem=halo_send.at[slot],
            recv_sem=halo_recv.at[slot],
            device_id={"seq": device},
        )

    @pl.when(me < n - 1)
    def _():
        halo_copy(0, me + 1).start()

    @pl.when(me > 0)
    def _():
        halo_copy(1, me - 1).start()

    square = (width, width)
    gain_column = jnp.sum(
        jnp.where(iota(square, 0) == iota(square, 1), norm_gain_ref[...], 0.0), axis=1, keepdims=True
    )

    def normed(values):
        mean_square = jnp.mean(values * values, axis=0, keepdims=True)
        return (values * lax.rsqrt(mean_square + EPSILON) * gain_column).astype(BF)

    edge = jnp.zeros((8, inner), F32)
    for a in range(3):
        pre[a, 0:8, :] = edge
        pre[a, tokens + 8 : tokens + 16, :] = edge
    own = mm_tn(normed(region_ref[...].astype(F32)), in_w_ref[...]).astype(BF)
    pre[1, 8 : tokens + 8, :] = own[:, :inner].astype(F32)
    gate[...] = own[:, inner:]

    @pl.when(me < n - 1)
    def _():
        halo_copy(1, me + 1).wait_recv()
        halo_copy(0, me + 1).wait_send()

    @pl.when(me == n - 1)
    def _():
        halo[1] = jnp.zeros((width, tokens), BF)

    @pl.when(me > 0)
    def _():
        halo_copy(0, me - 1).wait_recv()
        halo_copy(1, me - 1).wait_send()

    @pl.when(me == 0)
    def _():
        halo[0] = jnp.zeros((width, tokens), BF)

    for slot, a in ((0, 0), (1, 2)):
        rim = mm_tn(normed(halo[slot].astype(F32)), in_w_ref[:, :inner]).astype(BF)
        pre[a, 8 : tokens + 8, :] = rim.astype(F32)

    def a_copy(k, chunk, place):
        return pltpu.make_async_remote_copy(
            src_ref=act.at[chunk],
            dst_ref=colbuf.at[place],
            send_sem=a_send.at[k],
            recv_sem=a_recv.at[k],
            device_id={"seq": chunk},
        )

    per = TILE // band if band < TILE else 1
    for c in range(tokens // TILE):
        summed = conv_b_ref[...]
        for a in range(3):
            for b in range(3):
                first = c * TILE + 7 + b
                tap = 3 * a + b
                summed = summed + pre[a, first : first + TILE, :] * conv_w_ref[tap : tap + 1, :]
        done = (summed / (1.0 + jnp.exp(-summed))).astype(BF)
        if band <= TILE:
            act[c * per : (c + 1) * per] = done.reshape(per, band, inner)
        else:
            where = c * TILE // band
            start = c * TILE % band
            act[where, start : start + TILE] = done
        for d in range(c * TILE // band, (c + 1) * TILE // band):

            @pl.when(me != d)
            def _(d=d):
                a_copy(lax.rem(d - me + n, n), d, me).start()


    def s_copy(p, k, chunk, place):
        return pltpu.make_async_remote_copy(
            src_ref=msg.at[p, chunk],
            dst_ref=got.at[p, place],
            send_sem=s_send.at[p, k],
            recv_sem=s_recv.at[p, k],
            device_id={"seq": chunk},
        )

    def t_copy(p, k, chunk, place):
        return pltpu.make_async_remote_copy(
            src_ref=tot.at[p],
            dst_ref=got_tot.at[p, place],
            send_sem=t_send.at[p, k],
            recv_sem=t_recv.at[p, k],
            device_id={"seq": chunk},
        )

    def e_copy(p, k, chunk, place):
        return pltpu.make_async_remote_copy(
            src_ref=ent_out.at[p, chunk],
            dst_ref=ent_in.at[p, place],
            send_sem=e_send.at[p, k],
            recv_sem=e_recv.at[p, k],
            device_id={"seq": chunk},
        )

    def c_copy(k, chunk, place):
        return pltpu.make_async_remote_copy(
            src_ref=col_out.at[chunk],
            dst_ref=col_in.at[place],
            send_sem=c_send.at[k],
            recv_sem=c_recv.at[k],
            device_id={"seq": chunk},
        )

    def start_all(make):
        def one(k, _):
            make(k, peer_of(k), me).start()
            return 0

        lax.fori_loop(1, n, one, 0)

    def wait_all(make):
        def one(k, _):
            make(k, peer_of(k), source_of(k)).wait_recv()
            return 0

        lax.fori_loop(1, n, one, 0)

    def wait_sent(make):
        def one(k, _):
            make(k, peer_of(k), source_of(k)).wait_send()
            return 0

        lax.fori_loop(1, n, one, 0)

    colbuf[pl.ds(me, 1)] = act[pl.ds(me, 1)]

    group_lane = iota((1, groups), 1)
    behind_lane = lax.rem(group_lane, 2 * heads) >= heads
    lower = (iota((tokens, tokens), 0) >= iota((tokens, tokens), 1)).astype(BF)
    eye = (iota((groups, groups), 0) == iota((groups, groups), 1)).astype(BF)
    spread_row = iota((groups, inner), 0)
    spread_head = jnp.right_shift(iota((groups, inner), 1), head_bits)
    rates = -jnp.exp(decay_ref[...])

    def spreader(base):
        return (spread_row == base + spread_head).astype(F32)

    def expand(v, e):
        hi, mid, lo = (piece.astype(F32) for piece in split3(v))
        pieces = jnp.concatenate([hi, mid, lo], axis=1).astype(BF)
        return mm(pieces, jnp.concatenate([e, e, e], axis=0).astype(BF))

    def flip_axes(v):
        hi, mid, lo = split3(v)
        return mm_nt(eye, hi) + mm_nt(eye, mid) + mm_nt(eye, lo)

    def prepare(p, x):
        first = p * 4 * state
        coup[p] = mm(x, coup_w_ref[:, first : first + 4 * state]).astype(BF)
        logits = mm_nt(x, step_w_ref[...]) + step_b_ref[...]
        steps = jnp.maximum(logits, 0.0) + jnp.log1p(jnp.exp(-jnp.abs(logits)))
        logs = rates * steps
        hi, mid, lo = split3(logs)
        ahead = mm(lower, hi) + mm(lower, mid) + mm(lower, lo)
        total = ahead[tokens - 1 : tokens, :]
        c = jnp.where(behind_lane, total - ahead + logs, ahead)
        cum[p] = c
        cum_t[p] = flip_axes(c)
        step_t[p] = flip_axes(steps)
        tail = jnp.exp(total - c) * steps
        base = p * 2 * heads
        xf = x.astype(F32)
        spread_a, spread_b = spreader(base), spreader(base + heads)
        tot[p, :, 0:groups] = jnp.broadcast_to(total, (8, groups))
        start_all(functools.partial(t_copy, p))
        got_tot[p, pl.ds(me, 1)] = tot[p][None]
        contribs = []
        for o, e in ((0, spread_a), (1, spread_b)):
            weighted = (xf * expand(tail, e)).astype(BF)
            writer = coup[p, :, 2 * o * state : (2 * o + 1) * state]
            contribs.append(mm_tn(writer, weighted))
        for d in range(n):
            for o in range(2):
                msg[p, d, o * part : (o + 1) * part] = contribs[o][d * part : (d + 1) * part]
        start_all(functools.partial(s_copy, p))
        got[p, pl.ds(me, 1)] = msg[p, pl.ds(me, 1)]
        def diagonal(o):
            w = coup[p, :, 2 * o * state : (2 * o + 1) * state].astype(F32)
            r = coup[p, :, (2 * o + 1) * state : (2 * o + 2) * state].astype(F32)
            return jnp.sum(w * r, axis=-1, keepdims=True)

        diag = (jnp.where(behind_lane, diagonal(1), diagonal(0)) * steps).astype(BF).astype(F32)
        target = own_col if p else own_row
        target[...] = xf * expand(diag + skip_ref[...], spread_a + spread_b)
        even = jnp.bitwise_and(iota((1, inner), 1), head) == 0
        xe[...] = jnp.where(even, xf, 0.0).astype(BF)
        xo[...] = jnp.where(even, 0.0, xf).astype(BF)

    def mix(p, first, last):
        target = own_col if p else own_row

        def tile(i, _):
            t0 = pl.multiple_of(i * TILE, TILE)
            rows = pl.ds(t0, TILE)
            both = coup[p, rows, :]
            ahead = mm_nt(both[:, state : 2 * state], coup[p, :, 0:state])
            behind = mm_nt(both[:, 3 * state : 4 * state], coup[p, :, 2 * state : 3 * state])
            t = iota((TILE, tokens), 0) + t0
            s = iota((TILE, tokens), 1)
            after = t > s
            scores = jnp.where(after, ahead, jnp.where(t < s, behind, 0.0))
            c = cum[p, rows, :]

            def weights(h):
                f = p * 2 * heads + h
                g = f + heads
                lead = c[:, f : f + 1] - cum_t[p, f : f + 1, :]
                back = c[:, g : g + 1] - cum_t[p, g : g + 1, :]
                step = jnp.where(after, step_t[p, f : f + 1, :], step_t[p, g : g + 1, :])
                return (scores * jnp.exp(jnp.minimum(lead, back)) * step).astype(BF)

            for j in range(heads // 2):
                lanes = slice(2 * j * head, 2 * (j + 1) * head)
                inside = mm(weights(2 * j), xe[:, lanes]) + mm(weights(2 * j + 1), xo[:, lanes])
                target[rows, lanes] += inside
            return 0

        lax.fori_loop(first, last, tile, 0)

    def scan(p):
        wait_all(functools.partial(t_copy, p))
        base = p * 2 * heads
        totals = jnp.exp(
            jnp.concatenate([got_tot[p, i, 0:8, 0:groups] for i in range(n)], axis=0)
        )
        fade_a = expand(totals, spreader(base))
        fade_b = expand(totals, spreader(base + heads))
        wait_all(functools.partial(s_copy, p))
        entry = jnp.zeros((part, inner), F32)
        ahead = []
        for i in range(n):
            ahead.append(entry)
            entry = fade_a[8 * i : 8 * i + 1] * entry + got[p, i, 0:part, :]
        entry = jnp.zeros((part, inner), F32)
        for i in reversed(range(n)):
            pieces = [ahead[i], entry]
            if 2 * part < 16:
                pieces.append(jnp.zeros((16 - 2 * part, inner), F32))
            ent_out[p, i] = jnp.concatenate(pieces, axis=0).astype(BF)
            entry = fade_b[8 * i : 8 * i + 1] * entry + got[p, i, part : 2 * part, :]
        start_all(functools.partial(e_copy, p))
        ent_in[p, pl.ds(me, 1)] = ent_out[p, pl.ds(me, 1)]

    def finish(p):
        wait_all(functools.partial(e_copy, p))
        target = own_col if p else own_row
        arrived = [ent_in[p, i].astype(F32) for i in range(n)]
        grown = jnp.exp(cum[p])
        base = p * 2 * heads
        result = target[...]
        for o in range(2):
            entry = jnp.concatenate(
                [v[o * part : (o + 1) * part] for v in arrived], axis=0
            ).astype(BF)
            reader = coup[p, :, (2 * o + 1) * state : (2 * o + 2) * state]
            result = result + mm(reader, entry) * expand(grown, spreader(base + o * heads))
        return result

    x_row = act[...].reshape(tokens, inner)
    prepare(0, x_row)
    tiles = tokens // TILE
    mix(0, 0, tiles)
    wait_all(a_copy)
    place = iota((tokens, tokens), 0)
    cell = iota((tokens, tokens), 1)
    turn = cell == jnp.left_shift(jnp.bitwise_and(place, n - 1), band_bits) + jnp.right_shift(place, n_bits)
    xcol[...] = mm(turn.astype(BF), colbuf[...].reshape(tokens, inner)).astype(BF)
    prepare(1, xcol[...])
    scan(0)
    mix(1, 0, tiles // 2)
    scan(1)
    mix(1, tiles // 2, tiles)
    column = finish(1).astype(BF)
    back = cell == jnp.left_shift(jnp.bitwise_and(place, band - 1), n_bits) + jnp.right_shift(place, band_bits)
    col_out[...] = mm(back.astype(BF), column).astype(BF).reshape(n, band, inner)
    start_all(c_copy)
    col_in[pl.ds(me, 1)] = col_out[pl.ds(me, 1)]
    row_total = finish(0)
    g = gate[...].astype(F32)
    own_row[...] = row_total
    own_col[...] = g / (1.0 + jnp.exp(-g))
    wait_all(c_copy)
    for c in range(tokens // TILE):
        rows = slice(c * TILE, (c + 1) * TILE)
        if band <= TILE:
            col = col_in[c * per : (c + 1) * per].reshape(TILE, inner)
        else:
            start = c * TILE % band
            col = col_in[c * TILE // band, start : start + TILE]
        gated = (own_row[rows, :] + col.astype(F32)) * own_col[rows, :]
        mean_square = jnp.mean(gated * gated, axis=-1, keepdims=True)
        normy = (gated * lax.rsqrt(mean_square + EPSILON) * out_gain_ref[...]).astype(BF)
        out_ref[:, rows] = (
            region_ref[:, rows].astype(F32) + mm_nt(out_w_ref[...], normy)
        ).astype(BF)
    wait_sent(a_copy)
    for p in range(2):
        wait_sent(functools.partial(s_copy, p))
        wait_sent(functools.partial(t_copy, p))
        wait_sent(functools.partial(e_copy, p))
    wait_sent(c_copy)


def body(n, *args):
    region = args[0]
    rows, tokens, width = region.shape
    inner = args[11].shape[0]
    groups = args[7].shape[0]
    heads = groups // 4
    state = args[5].shape[1] // 8
    band = tokens // n
    part = state // n
    flat = [v if v.ndim > 1 else v.reshape(1, -1) for v in args]
    flat[0] = region[0].T
    flat[6] = flat[6].T
    flat[11] = flat[11].T
    ent_rows = max(16, 2 * part)
    dma = pltpu.SemaphoreType.DMA
    vmem = pltpu.VMEM
    refined = pl.pallas_call(
        functools.partial(kernel, n, heads, state),
        out_shape=jax.ShapeDtypeStruct((width, tokens), BF),
        in_specs=[pl.BlockSpec(memory_space=pltpu.VMEM)] * len(flat),
        out_specs=pl.BlockSpec(memory_space=pltpu.VMEM),
        scratch_shapes=[
            vmem((2, width, tokens), BF),
            vmem((3, tokens + 16, inner), F32),
            vmem((tokens, inner), BF),
            vmem((n, band, inner), BF),
            vmem((n, band, inner), BF),
            vmem((tokens, inner), BF),
            vmem((tokens, inner), BF),
            vmem((tokens, inner), BF),
            vmem((2, tokens, 4 * state), BF),
            vmem((2, tokens, groups), F32),
            vmem((2, groups, tokens), F32),
            vmem((2, groups, tokens), F32),
            vmem((tokens, inner), F32),
            vmem((tokens, inner), F32),
            vmem((2, n, 2 * part, inner), F32),
            vmem((2, n, 2 * part, inner), F32),
            vmem((2, 8, 128), F32),
            vmem((2, n, 8, 128), F32),
            vmem((2, n, ent_rows, inner), BF),
            vmem((2, n, ent_rows, inner), BF),
            vmem((n, band, inner), BF),
            vmem((n, band, inner), BF),
            dma((2,)),
            dma((2,)),
            dma((n,)),
            dma((n,)),
            dma((2, n)),
            dma((2, n)),
            dma((2, n)),
            dma((2, n)),
            dma((2, n)),
            dma((2, n)),
            dma((n,)),
            dma((n,)),
        ],
        compiler_params=pltpu.CompilerParams(
            collective_id=0, has_side_effects=True, vmem_limit_bytes=50 * 1024 * 1024
        ),
    )(*flat)
    return refined.T[None]


def solution(mesh):
    in_specs = (P(("dp", "seq"), None, None),) + (P(),) * 11
    return jax.shard_map(
        functools.partial(body, mesh.shape["seq"]),
        mesh=mesh,
        in_specs=in_specs,
        out_specs=P(("dp", "seq"), None, None),
        check_vma=False,
    )
```

```python
import functools
import jax
import jax.numpy as jnp
from jax import lax
from jax.experimental import pallas as pl
from jax.experimental.pallas import tpu as pltpu
from jax.sharding import PartitionSpec as P

EPSILON = 1e-05
BF = jnp.bfloat16
F32 = jnp.float32
TILE = 128


def mm(a, b):
    return jnp.dot(a, b, preferred_element_type=F32)


def mm_nt(a, b):
    return lax.dot_general(a, b, (((1,), (1,)), ((), ())), preferred_element_type=F32)


def mm_tn(a, b):
    return lax.dot_general(a, b, (((0,), (0,)), ((), ())), preferred_element_type=F32)


def split3(v):
    hi = v.astype(BF)
    rest = v - hi.astype(F32)
    mid = rest.astype(BF)
    lo = (rest - mid.astype(F32)).astype(BF)
    return hi, mid, lo


def iota(shape, dim):
    return lax.broadcasted_iota(jnp.int32, shape, dim)


def kernel(
    n,
    heads,
    state,
    region_ref,
    norm_gain_ref,
    in_w_ref,
    conv_w_ref,
    conv_b_ref,
    coup_w_ref,
    step_w_ref,
    step_b_ref,
    decay_ref,
    skip_ref,
    out_gain_ref,
    out_w_ref,
    out_ref,
    halo,
    pre,
    gate,
    act,
    colbuf,
    xcol,
    xe,
    xo,
    coup,
    cum,
    cum_t,
    step_t,
    own_row,
    own_col,
    msg,
    got,
    tot,
    got_tot,
    ent_out,
    ent_in,
    col_out,
    col_in,
    halo_send,
    halo_recv,
    a_send,
    a_recv,
    s_send,
    s_recv,
    t_send,
    t_recv,
    e_send,
    e_recv,
    c_send,
    c_recv,
):
    me = lax.axis_index("seq")
    width, tokens = region_ref.shape
    inner = out_w_ref.shape[1]
    band = tokens // n
    head = inner // heads
    part = state // n
    head_bits = head.bit_length() - 1
    n_bits = n.bit_length() - 1
    band_bits = band.bit_length() - 1
    groups = 4 * heads

    def peer_of(k):
        return lax.rem(me + k, n)

    def source_of(k):
        return lax.rem(me + n - k, n)

    barrier = pltpu.get_barrier_semaphore()

    def greet(k, _):
        pl.semaphore_signal(barrier, inc=1, device_id={"seq": peer_of(k)})
        return 0

    lax.fori_loop(1, n, greet, 0)
    pl.semaphore_wait(barrier, n - 1)

    def halo_copy(slot, device):
        return pltpu.make_async_remote_copy(
            src_ref=region_ref,
            dst_ref=halo.at[slot],
            send_sem=halo_send.at[slot],
            recv_sem=halo_recv.at[slot],
            device_id={"seq": device},
        )

    @pl.when(me < n - 1)
    def _():
        halo_copy(0, me + 1).start()

    @pl.when(me > 0)
    def _():
        halo_copy(1, me - 1).start()

    square = (width, width)
    gain_column = jnp.sum(
        jnp.where(iota(square, 0) == iota(square, 1), norm_gain_ref[...], 0.0), axis=1, keepdims=True
    )

    def normed(values):
        mean_square = jnp.mean(values * values, axis=0, keepdims=True)
        return (values * lax.rsqrt(mean_square + EPSILON) * gain_column).astype(BF)

    edge = jnp.zeros((8, inner), F32)
    for a in range(3):
        pre[a, 0:8, :] = edge
        pre[a, tokens + 8 : tokens + 16, :] = edge
    own = mm_tn(normed(region_ref[...].astype(F32)), in_w_ref[...]).astype(BF)
    pre[1, 8 : tokens + 8, :] = own[:, :inner].astype(F32)
    gate[...] = own[:, inner:]

    @pl.when(me < n - 1)
    def _():
        halo_copy(1, me + 1).wait_recv()
        halo_copy(0, me + 1).wait_send()

    @pl.when(me == n - 1)
    def _():
        halo[1] = jnp.zeros((width, tokens), BF)

    @pl.when(me > 0)
    def _():
        halo_copy(0, me - 1).wait_recv()
        halo_copy(1, me - 1).wait_send()

    @pl.when(me == 0)
    def _():
        halo[0] = jnp.zeros((width, tokens), BF)

    for slot, a in ((0, 0), (1, 2)):
        rim = mm_tn(normed(halo[slot].astype(F32)), in_w_ref[:, :inner]).astype(BF)
        pre[a, 8 : tokens + 8, :] = rim.astype(F32)

    def a_copy(k, chunk, place):
        return pltpu.make_async_remote_copy(
            src_ref=act.at[chunk],
            dst_ref=colbuf.at[place],
            send_sem=a_send.at[k],
            recv_sem=a_recv.at[k],
            device_id={"seq": chunk},
        )

    per = TILE // band if band < TILE else 1
    for c in range(tokens // TILE):
        summed = conv_b_ref[...]
        for a in range(3):
            for b in range(3):
                first = c * TILE + 7 + b
                tap = 3 * a + b
                summed = summed + pre[a, first : first + TILE, :] * conv_w_ref[tap : tap + 1, :]
        done = (summed / (1.0 + jnp.exp(-summed))).astype(BF)
        if band <= TILE:
            act[c * per : (c + 1) * per] = done.reshape(per, band, inner)
        else:
            where = c * TILE // band
            start = c * TILE % band
            act[where, start : start + TILE] = done
        for d in range(c * TILE // band, (c + 1) * TILE // band):

            @pl.when(me != d)
            def _(d=d):
                a_copy(lax.rem(d - me + n, n), d, me).start()


    def s_copy(p, k, chunk, place):
        return pltpu.make_async_remote_copy(
            src_ref=msg.at[p, chunk],
            dst_ref=got.at[p, place],
            send_sem=s_send.at[p, k],
            recv_sem=s_recv.at[p, k],
            device_id={"seq": chunk},
        )

    def t_copy(p, k, chunk, place):
        return pltpu.make_async_remote_copy(
            src_ref=tot.at[p],
            dst_ref=got_tot.at[p, place],
            send_sem=t_send.at[p, k],
            recv_sem=t_recv.at[p, k],
            device_id={"seq": chunk},
        )

    def e_copy(p, k, chunk, place):
        return pltpu.make_async_remote_copy(
            src_ref=ent_out.at[p, chunk],
            dst_ref=ent_in.at[p, place],
            send_sem=e_send.at[p, k],
            recv_sem=e_recv.at[p, k],
            device_id={"seq": chunk},
        )

    def c_copy(k, chunk, place):
        return pltpu.make_async_remote_copy(
            src_ref=col_out.at[chunk],
            dst_ref=col_in.at[place],
            send_sem=c_send.at[k],
            recv_sem=c_recv.at[k],
            device_id={"seq": chunk},
        )

    def start_all(make):
        def one(k, _):
            make(k, peer_of(k), me).start()
            return 0

        lax.fori_loop(1, n, one, 0)

    def wait_all(make):
        def one(k, _):
            make(k, peer_of(k), source_of(k)).wait_recv()
            return 0

        lax.fori_loop(1, n, one, 0)

    def wait_sent(make):
        def one(k, _):
            make(k, peer_of(k), source_of(k)).wait_send()
            return 0

        lax.fori_loop(1, n, one, 0)

    colbuf[pl.ds(me, 1)] = act[pl.ds(me, 1)]

    group_lane = iota((1, groups), 1)
    behind_lane = lax.rem(group_lane, 2 * heads) >= heads
    lower = (iota((tokens, tokens), 0) >= iota((tokens, tokens), 1)).astype(BF)
    eye = (iota((groups, groups), 0) == iota((groups, groups), 1)).astype(BF)
    spread_row = iota((groups, inner), 0)
    spread_head = jnp.right_shift(iota((groups, inner), 1), head_bits)
    rates = -jnp.exp(decay_ref[...])

    def spreader(base):
        return (spread_row == base + spread_head).astype(F32)

    def expand(v, e):
        hi, mid, lo = (piece.astype(F32) for piece in split3(v))
        pieces = jnp.concatenate([hi, mid, lo], axis=1).astype(BF)
        return mm(pieces, jnp.concatenate([e, e, e], axis=0).astype(BF))

    def flip_axes(v):
        hi, mid, lo = split3(v)
        return mm_nt(eye, hi) + mm_nt(eye, mid) + mm_nt(eye, lo)

    def prepare(p, x):
        first = p * 4 * state
        coup[p] = mm(x, coup_w_ref[:, first : first + 4 * state]).astype(BF)
        logits = mm_nt(x, step_w_ref[...]) + step_b_ref[...]
        steps = jnp.maximum(logits, 0.0) + jnp.log1p(jnp.exp(-jnp.abs(logits)))
        logs = rates * steps
        hi, mid, lo = split3(logs)
        ahead = mm(lower, hi) + mm(lower, mid) + mm(lower, lo)
        total = ahead[tokens - 1 : tokens, :]
        c = jnp.where(behind_lane, total - ahead + logs, ahead)
        cum[p] = c
        tail = jnp.exp(total - c) * steps
        base = p * 2 * heads
        xf = x.astype(F32)
        spread_a, spread_b = spreader(base), spreader(base + heads)
        tot[p, :, 0:groups] = jnp.broadcast_to(total, (8, groups))
        start_all(functools.partial(t_copy, p))
        got_tot[p, pl.ds(me, 1)] = tot[p][None]
        contribs = []
        for o, e in ((0, spread_a), (1, spread_b)):
            weighted = (xf * expand(tail, e)).astype(BF)
            writer = coup[p, :, 2 * o * state : (2 * o + 1) * state]
            contribs.append(mm_tn(writer, weighted))
        for d in range(n):
            for o in range(2):
                msg[p, d, o * part : (o + 1) * part] = contribs[o][d * part : (d + 1) * part]
        if p == 1:
            start_all(functools.partial(s_copy, p))
        cum_t[p] = flip_axes(c)
        step_t[p] = flip_axes(steps)
        got[p, pl.ds(me, 1)] = msg[p, pl.ds(me, 1)]
        def diagonal(o):
            w = coup[p, :, 2 * o * state : (2 * o + 1) * state].astype(F32)
            r = coup[p, :, (2 * o + 1) * state : (2 * o + 2) * state].astype(F32)
            return jnp.sum(w * r, axis=-1, keepdims=True)

        diag = (jnp.where(behind_lane, diagonal(1), diagonal(0)) * steps).astype(BF).astype(F32)
        target = own_col if p else own_row
        target[...] = xf * expand(diag + skip_ref[...], spread_a + spread_b)
        even = jnp.bitwise_and(iota((1, inner), 1), head) == 0
        xe[...] = jnp.where(even, xf, 0.0).astype(BF)
        xo[...] = jnp.where(even, 0.0, xf).astype(BF)

    def mix(p, first, last):
        target = own_col if p else own_row

        def tile(i, _):
            t0 = pl.multiple_of(i * TILE, TILE)
            rows = pl.ds(t0, TILE)
            both = coup[p, rows, :]
            ahead = mm_nt(both[:, state : 2 * state], coup[p, :, 0:state])
            behind = mm_nt(both[:, 3 * state : 4 * state], coup[p, :, 2 * state : 3 * state])
            t = iota((TILE, tokens), 0) + t0
            s = iota((TILE, tokens), 1)
            after = t > s
            scores = jnp.where(after, ahead, jnp.where(t < s, behind, 0.0))
            c = cum[p, rows, :]

            def weights(h):
                f = p * 2 * heads + h
                g = f + heads
                lead = c[:, f : f + 1] - cum_t[p, f : f + 1, :]
                back = c[:, g : g + 1] - cum_t[p, g : g + 1, :]
                step = jnp.where(after, step_t[p, f : f + 1, :], step_t[p, g : g + 1, :])
                return (scores * jnp.exp(jnp.minimum(lead, back)) * step).astype(BF)

            for j in range(heads // 2):
                lanes = slice(2 * j * head, 2 * (j + 1) * head)
                inside = mm(weights(2 * j), xe[:, lanes]) + mm(weights(2 * j + 1), xo[:, lanes])
                target[rows, lanes] += inside
            return 0

        lax.fori_loop(first, last, tile, 0)

    def scan(p):
        wait_all(functools.partial(t_copy, p))
        base = p * 2 * heads
        totals = jnp.exp(
            jnp.concatenate([got_tot[p, i, 0:8, 0:groups] for i in range(n)], axis=0)
        )
        fade_a = expand(totals, spreader(base))
        fade_b = expand(totals, spreader(base + heads))
        wait_all(functools.partial(s_copy, p))
        entry = jnp.zeros((part, inner), F32)
        ahead = []
        for i in range(n):
            ahead.append(entry)
            entry = fade_a[8 * i : 8 * i + 1] * entry + got[p, i, 0:part, :]
        entry = jnp.zeros((part, inner), F32)
        for i in reversed(range(n)):
            pieces = [ahead[i], entry]
            if 2 * part < 16:
                pieces.append(jnp.zeros((16 - 2 * part, inner), F32))
            ent_out[p, i] = jnp.concatenate(pieces, axis=0).astype(BF)
            entry = fade_b[8 * i : 8 * i + 1] * entry + got[p, i, part : 2 * part, :]
        start_all(functools.partial(e_copy, p))
        ent_in[p, pl.ds(me, 1)] = ent_out[p, pl.ds(me, 1)]

    def finish(p):
        wait_all(functools.partial(e_copy, p))
        target = own_col if p else own_row
        arrived = [ent_in[p, i].astype(F32) for i in range(n)]
        grown = jnp.exp(cum[p])
        base = p * 2 * heads
        result = target[...]
        for o in range(2):
            entry = jnp.concatenate(
                [v[o * part : (o + 1) * part] for v in arrived], axis=0
            ).astype(BF)
            reader = coup[p, :, (2 * o + 1) * state : (2 * o + 2) * state]
            result = result + mm(reader, entry) * expand(grown, spreader(base + o * heads))
        return result

    x_row = act[...].reshape(tokens, inner)
    prepare(0, x_row)
    tiles = tokens // TILE
    mix(0, 0, tiles)
    wait_all(a_copy)
    start_all(functools.partial(s_copy, 0))
    place = iota((tokens, tokens), 0)
    cell = iota((tokens, tokens), 1)
    turn = cell == jnp.left_shift(jnp.bitwise_and(place, n - 1), band_bits) + jnp.right_shift(place, n_bits)
    xcol[...] = mm(turn.astype(BF), colbuf[...].reshape(tokens, inner)).astype(BF)
    prepare(1, xcol[...])
    mix(1, 0, tiles // 2)
    scan(1)
    scan(0)
    mix(1, tiles // 2, tiles)
    column = finish(1).astype(BF)
    back = cell == jnp.left_shift(jnp.bitwise_and(place, band - 1), n_bits) + jnp.right_shift(place, band_bits)
    col_out[...] = mm(back.astype(BF), column).astype(BF).reshape(n, band, inner)
    start_all(c_copy)
    col_in[pl.ds(me, 1)] = col_out[pl.ds(me, 1)]
    row_total = finish(0)
    g = gate[...].astype(F32)
    own_row[...] = row_total
    own_col[...] = g / (1.0 + jnp.exp(-g))
    wait_all(c_copy)
    for c in range(tokens // TILE):
        rows = slice(c * TILE, (c + 1) * TILE)
        if band <= TILE:
            col = col_in[c * per : (c + 1) * per].reshape(TILE, inner)
        else:
            start = c * TILE % band
            col = col_in[c * TILE // band, start : start + TILE]
        gated = (own_row[rows, :] + col.astype(F32)) * own_col[rows, :]
        mean_square = jnp.mean(gated * gated, axis=-1, keepdims=True)
        normy = (gated * lax.rsqrt(mean_square + EPSILON) * out_gain_ref[...]).astype(BF)
        out_ref[:, rows] = (
            region_ref[:, rows].astype(F32) + mm_nt(out_w_ref[...], normy)
        ).astype(BF)
    wait_sent(a_copy)
    for p in range(2):
        wait_sent(functools.partial(s_copy, p))
        wait_sent(functools.partial(t_copy, p))
        wait_sent(functools.partial(e_copy, p))
    wait_sent(c_copy)


def body(n, *args):
    region = args[0]
    rows, tokens, width = region.shape
    inner = args[11].shape[0]
    groups = args[7].shape[0]
    heads = groups // 4
    state = args[5].shape[1] // 8
    band = tokens // n
    part = state // n
    flat = [v if v.ndim > 1 else v.reshape(1, -1) for v in args]
    flat[0] = region[0].T
    flat[6] = flat[6].T
    flat[11] = flat[11].T
    ent_rows = max(16, 2 * part)
    dma = pltpu.SemaphoreType.DMA
    vmem = pltpu.VMEM
    refined = pl.pallas_call(
        functools.partial(kernel, n, heads, state),
        out_shape=jax.ShapeDtypeStruct((width, tokens), BF),
        in_specs=[pl.BlockSpec(memory_space=pltpu.VMEM)] * len(flat),
        out_specs=pl.BlockSpec(memory_space=pltpu.VMEM),
        scratch_shapes=[
            vmem((2, width, tokens), BF),
            vmem((3, tokens + 16, inner), F32),
            vmem((tokens, inner), BF),
            vmem((n, band, inner), BF),
            vmem((n, band, inner), BF),
            vmem((tokens, inner), BF),
            vmem((tokens, inner), BF),
            vmem((tokens, inner), BF),
            vmem((2, tokens, 4 * state), BF),
            vmem((2, tokens, groups), F32),
            vmem((2, groups, tokens), F32),
            vmem((2, groups, tokens), F32),
            vmem((tokens, inner), F32),
            vmem((tokens, inner), F32),
            vmem((2, n, 2 * part, inner), F32),
            vmem((2, n, 2 * part, inner), F32),
            vmem((2, 8, 128), F32),
            vmem((2, n, 8, 128), F32),
            vmem((2, n, ent_rows, inner), BF),
            vmem((2, n, ent_rows, inner), BF),
            vmem((n, band, inner), BF),
            vmem((n, band, inner), BF),
            dma((2,)),
            dma((2,)),
            dma((n,)),
            dma((n,)),
            dma((2, n)),
            dma((2, n)),
            dma((2, n)),
            dma((2, n)),
            dma((2, n)),
            dma((2, n)),
            dma((n,)),
            dma((n,)),
        ],
        compiler_params=pltpu.CompilerParams(
            collective_id=0, has_side_effects=True, vmem_limit_bytes=50 * 1024 * 1024
        ),
    )(*flat)
    return refined.T[None]


def solution(mesh):
    in_specs = (P(("dp", "seq"), None, None),) + (P(),) * 11
    return jax.shard_map(
        functools.partial(body, mesh.shape["seq"]),
        mesh=mesh,
        in_specs=in_specs,
        out_specs=P(("dp", "seq"), None, None),
        check_vma=False,
    )
```

```python
import functools
import jax
import jax.numpy as jnp
from jax import lax
from jax.experimental import pallas as pl
from jax.experimental.pallas import tpu as pltpu
from jax.sharding import PartitionSpec as P

EPSILON = 1e-05
BF = jnp.bfloat16
F32 = jnp.float32
TILE = 128


def mm(a, b):
    return jnp.dot(a, b, preferred_element_type=F32)


def mm_nt(a, b):
    return lax.dot_general(a, b, (((1,), (1,)), ((), ())), preferred_element_type=F32)


def mm_tn(a, b):
    return lax.dot_general(a, b, (((0,), (0,)), ((), ())), preferred_element_type=F32)


def split3(v):
    hi = v.astype(BF)
    rest = v - hi.astype(F32)
    mid = rest.astype(BF)
    lo = (rest - mid.astype(F32)).astype(BF)
    return hi, mid, lo


def iota(shape, dim):
    return lax.broadcasted_iota(jnp.int32, shape, dim)


def kernel(
    n,
    heads,
    state,
    region_ref,
    norm_gain_ref,
    in_w_ref,
    conv_w_ref,
    conv_b_ref,
    coup_w_ref,
    step_w_ref,
    step_b_ref,
    decay_ref,
    skip_ref,
    out_gain_ref,
    out_w_ref,
    out_ref,
    halo,
    pre,
    gate,
    act,
    colbuf,
    xcol,
    xe,
    xo,
    coup,
    cum,
    cum_t,
    step_t,
    own_row,
    own_col,
    msg,
    got,
    tot,
    got_tot,
    ent_out,
    ent_in,
    col_out,
    col_in,
    halo_send,
    halo_recv,
    a_send,
    a_recv,
    s_send,
    s_recv,
    t_send,
    t_recv,
    e_send,
    e_recv,
    c_send,
    c_recv,
):
    me = lax.axis_index("seq")
    width, tokens = region_ref.shape
    inner = out_w_ref.shape[1]
    band = tokens // n
    head = inner // heads
    part = state // n
    head_bits = head.bit_length() - 1
    n_bits = n.bit_length() - 1
    band_bits = band.bit_length() - 1
    groups = 4 * heads

    def peer_of(k):
        return lax.rem(me + k, n)

    def source_of(k):
        return lax.rem(me + n - k, n)

    barrier = pltpu.get_barrier_semaphore()

    def greet(k, _):
        pl.semaphore_signal(barrier, inc=1, device_id={"seq": peer_of(k)})
        return 0

    lax.fori_loop(1, n, greet, 0)
    pl.semaphore_wait(barrier, n - 1)

    tiles = tokens // TILE

    def halo_copy(slot, c, device):
        cells = pl.ds(c * TILE, TILE)
        return pltpu.make_async_remote_copy(
            src_ref=region_ref.at[:, cells],
            dst_ref=halo.at[slot, :, cells],
            send_sem=halo_send.at[slot, c],
            recv_sem=halo_recv.at[slot, c],
            device_id={"seq": device},
        )

    for c in range(tiles):

        @pl.when(me < n - 1)
        def _(c=c):
            halo_copy(0, c, me + 1).start()

        @pl.when(me > 0)
        def _(c=c):
            halo_copy(1, c, me - 1).start()

    @pl.when(me == n - 1)
    def _():
        halo[1] = jnp.zeros((width, tokens), BF)

    @pl.when(me == 0)
    def _():
        halo[0] = jnp.zeros((width, tokens), BF)

    square = (width, width)
    gain_column = jnp.sum(
        jnp.where(iota(square, 0) == iota(square, 1), norm_gain_ref[...], 0.0), axis=1, keepdims=True
    )

    def normed(values):
        mean_square = jnp.mean(values * values, axis=0, keepdims=True)
        return (values * lax.rsqrt(mean_square + EPSILON) * gain_column).astype(BF)

    edge = jnp.zeros((8, inner), F32)
    for a in range(3):
        pre[a, 0:8, :] = edge
        pre[a, tokens + 8 : tokens + 16, :] = edge
    own = normed(region_ref[...].astype(F32))
    pre[1, 8 : tokens + 8, :] = mm_tn(own, in_w_ref[:, :inner]).astype(BF).astype(F32)

    def a_copy(k, chunk, place):
        return pltpu.make_async_remote_copy(
            src_ref=act.at[chunk],
            dst_ref=colbuf.at[place],
            send_sem=a_send.at[k],
            recv_sem=a_recv.at[k],
            device_id={"seq": chunk},
        )

    per = TILE // band if band < TILE else 1
    def convolve(c):
        summed = conv_b_ref[...]
        for a in range(3):
            for b in range(3):
                first = c * TILE + 7 + b
                tap = 3 * a + b
                summed = summed + pre[a, first : first + TILE, :] * conv_w_ref[tap : tap + 1, :]
        done = (summed / (1.0 + jnp.exp(-summed))).astype(BF)
        if band <= TILE:
            act[c * per : (c + 1) * per] = done.reshape(per, band, inner)
        else:
            where = c * TILE // band
            start = c * TILE % band
            act[where, start : start + TILE] = done
        for d in range(c * TILE // band, (c + 1) * TILE // band):

            @pl.when(me != d)
            def _(d=d):
                a_copy(lax.rem(d - me + n, n), d, me).start()


    for c in range(tiles + 1):
        if c < tiles:

            @pl.when(me < n - 1)
            def _(c=c):
                halo_copy(1, c, me + 1).wait_recv()

            @pl.when(me > 0)
            def _(c=c):
                halo_copy(0, c, me - 1).wait_recv()

            cells = slice(c * TILE, (c + 1) * TILE)
            for slot, a in ((0, 0), (1, 2)):
                rim = mm_tn(normed(halo[slot, :, cells].astype(F32)), in_w_ref[:, :inner])
                pre[a, 8 + c * TILE : 8 + (c + 1) * TILE, :] = rim.astype(BF).astype(F32)
        if c > 0:
            convolve(c - 1)

    gate[...] = mm_tn(own, in_w_ref[:, inner:]).astype(BF)

    def s_copy(p, k, chunk, place):
        return pltpu.make_async_remote_copy(
            src_ref=msg.at[p, chunk],
            dst_ref=got.at[p, place],
            send_sem=s_send.at[p, k],
            recv_sem=s_recv.at[p, k],
            device_id={"seq": chunk},
        )

    def t_copy(p, k, chunk, place):
        return pltpu.make_async_remote_copy(
            src_ref=tot.at[p],
            dst_ref=got_tot.at[p, place],
            send_sem=t_send.at[p, k],
            recv_sem=t_recv.at[p, k],
            device_id={"seq": chunk},
        )

    def e_copy(p, k, chunk, place):
        return pltpu.make_async_remote_copy(
            src_ref=ent_out.at[p, chunk],
            dst_ref=ent_in.at[p, place],
            send_sem=e_send.at[p, k],
            recv_sem=e_recv.at[p, k],
            device_id={"seq": chunk},
        )

    def c_copy(k, chunk, place):
        return pltpu.make_async_remote_copy(
            src_ref=col_out.at[chunk],
            dst_ref=col_in.at[place],
            send_sem=c_send.at[k],
            recv_sem=c_recv.at[k],
            device_id={"seq": chunk},
        )

    def start_all(make):
        def one(k, _):
            make(k, peer_of(k), me).start()
            return 0

        lax.fori_loop(1, n, one, 0)

    def wait_all(make):
        def one(k, _):
            make(k, peer_of(k), source_of(k)).wait_recv()
            return 0

        lax.fori_loop(1, n, one, 0)

    def wait_sent(make):
        def one(k, _):
            make(k, peer_of(k), source_of(k)).wait_send()
            return 0

        lax.fori_loop(1, n, one, 0)

    colbuf[pl.ds(me, 1)] = act[pl.ds(me, 1)]

    group_lane = iota((1, groups), 1)
    behind_lane = lax.rem(group_lane, 2 * heads) >= heads
    lower = (iota((tokens, tokens), 0) >= iota((tokens, tokens), 1)).astype(BF)
    eye = (iota((groups, groups), 0) == iota((groups, groups), 1)).astype(BF)
    spread_row = iota((groups, inner), 0)
    spread_head = jnp.right_shift(iota((groups, inner), 1), head_bits)
    rates = -jnp.exp(decay_ref[...])

    def spreader(base):
        return (spread_row == base + spread_head).astype(F32)

    def expand(v, e):
        hi, mid, lo = (piece.astype(F32) for piece in split3(v))
        pieces = jnp.concatenate([hi, mid, lo], axis=1).astype(BF)
        return mm(pieces, jnp.concatenate([e, e, e], axis=0).astype(BF))

    def flip_axes(v):
        hi, mid, lo = split3(v)
        return mm_nt(eye, hi) + mm_nt(eye, mid) + mm_nt(eye, lo)

    def prepare(p, x):
        first = p * 4 * state
        coup[p] = mm(x, coup_w_ref[:, first : first + 4 * state]).astype(BF)
        logits = mm_nt(x, step_w_ref[...]) + step_b_ref[...]
        steps = jnp.maximum(logits, 0.0) + jnp.log1p(jnp.exp(-jnp.abs(logits)))
        logs = rates * steps
        hi, mid, lo = split3(logs)
        ahead = mm(lower, hi) + mm(lower, mid) + mm(lower, lo)
        total = ahead[tokens - 1 : tokens, :]
        c = jnp.where(behind_lane, total - ahead + logs, ahead)
        cum[p] = c
        tail = jnp.exp(total - c) * steps
        base = p * 2 * heads
        xf = x.astype(F32)
        spread_a, spread_b = spreader(base), spreader(base + heads)
        tot[p, :, 0:groups] = jnp.broadcast_to(total, (8, groups))
        start_all(functools.partial(t_copy, p))
        got_tot[p, pl.ds(me, 1)] = tot[p][None]
        contribs = []
        for o, e in ((0, spread_a), (1, spread_b)):
            weighted = (xf * expand(tail, e)).astype(BF)
            writer = coup[p, :, 2 * o * state : (2 * o + 1) * state]
            contribs.append(mm_tn(writer, weighted))
        for d in range(n):
            for o in range(2):
                msg[p, d, o * part : (o + 1) * part] = contribs[o][d * part : (d + 1) * part]
        if p == 1:
            start_all(functools.partial(s_copy, p))
        cum_t[p] = flip_axes(c)
        step_t[p] = flip_axes(steps)
        got[p, pl.ds(me, 1)] = msg[p, pl.ds(me, 1)]
        def diagonal(o):
            w = coup[p, :, 2 * o * state : (2 * o + 1) * state].astype(F32)
            r = coup[p, :, (2 * o + 1) * state : (2 * o + 2) * state].astype(F32)
            return jnp.sum(w * r, axis=-1, keepdims=True)

        diag = (jnp.where(behind_lane, diagonal(1), diagonal(0)) * steps).astype(BF).astype(F32)
        target = own_col if p else own_row
        target[...] = xf * expand(diag + skip_ref[...], spread_a + spread_b)
        even = jnp.bitwise_and(iota((1, inner), 1), head) == 0
        xe[...] = jnp.where(even, xf, 0.0).astype(BF)
        xo[...] = jnp.where(even, 0.0, xf).astype(BF)

    def mix(p, first, last):
        target = own_col if p else own_row

        def tile(i, _):
            t0 = pl.multiple_of(i * TILE, TILE)
            rows = pl.ds(t0, TILE)
            both = coup[p, rows, :]
            ahead = mm_nt(both[:, state : 2 * state], coup[p, :, 0:state])
            behind = mm_nt(both[:, 3 * state : 4 * state], coup[p, :, 2 * state : 3 * state])
            t = iota((TILE, tokens), 0) + t0
            s = iota((TILE, tokens), 1)
            after = t > s
            scores = jnp.where(after, ahead, jnp.where(t < s, behind, 0.0))
            c = cum[p, rows, :]

            def weights(h):
                f = p * 2 * heads + h
                g = f + heads
                lead = c[:, f : f + 1] - cum_t[p, f : f + 1, :]
                back = c[:, g : g + 1] - cum_t[p, g : g + 1, :]
                step = jnp.where(after, step_t[p, f : f + 1, :], step_t[p, g : g + 1, :])
                return (scores * jnp.exp(jnp.minimum(lead, back)) * step).astype(BF)

            for j in range(heads // 2):
                lanes = slice(2 * j * head, 2 * (j + 1) * head)
                inside = mm(weights(2 * j), xe[:, lanes]) + mm(weights(2 * j + 1), xo[:, lanes])
                target[rows, lanes] += inside
            return 0

        lax.fori_loop(first, last, tile, 0)

    def scan(p):
        wait_all(functools.partial(t_copy, p))
        base = p * 2 * heads
        totals = jnp.exp(
            jnp.concatenate([got_tot[p, i, 0:8, 0:groups] for i in range(n)], axis=0)
        )
        fade_a = expand(totals, spreader(base))
        fade_b = expand(totals, spreader(base + heads))
        wait_all(functools.partial(s_copy, p))
        entry = jnp.zeros((part, inner), F32)
        ahead = []
        for i in range(n):
            ahead.append(entry)
            entry = fade_a[8 * i : 8 * i + 1] * entry + got[p, i, 0:part, :]
        entry = jnp.zeros((part, inner), F32)
        for i in reversed(range(n)):
            pieces = [ahead[i], entry]
            if 2 * part < 16:
                pieces.append(jnp.zeros((16 - 2 * part, inner), F32))
            ent_out[p, i] = jnp.concatenate(pieces, axis=0).astype(BF)
            entry = fade_b[8 * i : 8 * i + 1] * entry + got[p, i, part : 2 * part, :]
        start_all(functools.partial(e_copy, p))
        ent_in[p, pl.ds(me, 1)] = ent_out[p, pl.ds(me, 1)]

    def finish(p):
        wait_all(functools.partial(e_copy, p))
        target = own_col if p else own_row
        arrived = [ent_in[p, i].astype(F32) for i in range(n)]
        grown = jnp.exp(cum[p])
        base = p * 2 * heads
        result = target[...]
        for o in range(2):
            entry = jnp.concatenate(
                [v[o * part : (o + 1) * part] for v in arrived], axis=0
            ).astype(BF)
            reader = coup[p, :, (2 * o + 1) * state : (2 * o + 2) * state]
            result = result + mm(reader, entry) * expand(grown, spreader(base + o * heads))
        return result

    x_row = act[...].reshape(tokens, inner)
    prepare(0, x_row)
    mix(0, 0, tiles)
    wait_all(a_copy)
    start_all(functools.partial(s_copy, 0))
    place = iota((tokens, tokens), 0)
    cell = iota((tokens, tokens), 1)
    turn = cell == jnp.left_shift(jnp.bitwise_and(place, n - 1), band_bits) + jnp.right_shift(place, n_bits)
    xcol[...] = mm(turn.astype(BF), colbuf[...].reshape(tokens, inner)).astype(BF)
    prepare(1, xcol[...])
    mix(1, 0, tiles // 2)
    scan(1)
    scan(0)
    mix(1, tiles // 2, tiles)
    column = finish(1).astype(BF)
    back = cell == jnp.left_shift(jnp.bitwise_and(place, band - 1), n_bits) + jnp.right_shift(place, band_bits)
    col_out[...] = mm(back.astype(BF), column).astype(BF).reshape(n, band, inner)
    start_all(c_copy)
    col_in[pl.ds(me, 1)] = col_out[pl.ds(me, 1)]
    row_total = finish(0)
    g = gate[...].astype(F32)
    own_row[...] = row_total
    own_col[...] = g / (1.0 + jnp.exp(-g))
    wait_all(c_copy)
    for c in range(tokens // TILE):
        rows = slice(c * TILE, (c + 1) * TILE)
        if band <= TILE:
            col = col_in[c * per : (c + 1) * per].reshape(TILE, inner)
        else:
            start = c * TILE % band
            col = col_in[c * TILE // band, start : start + TILE]
        gated = (own_row[rows, :] + col.astype(F32)) * own_col[rows, :]
        mean_square = jnp.mean(gated * gated, axis=-1, keepdims=True)
        normy = (gated * lax.rsqrt(mean_square + EPSILON) * out_gain_ref[...]).astype(BF)
        out_ref[:, rows] = (
            region_ref[:, rows].astype(F32) + mm_nt(out_w_ref[...], normy)
        ).astype(BF)
    for c in range(tiles):

        @pl.when(me < n - 1)
        def _(c=c):
            halo_copy(0, c, me + 1).wait_send()

        @pl.when(me > 0)
        def _(c=c):
            halo_copy(1, c, me - 1).wait_send()

    wait_sent(a_copy)
    for p in range(2):
        wait_sent(functools.partial(s_copy, p))
        wait_sent(functools.partial(t_copy, p))
        wait_sent(functools.partial(e_copy, p))
    wait_sent(c_copy)


def body(n, *args):
    region = args[0]
    rows, tokens, width = region.shape
    inner = args[11].shape[0]
    groups = args[7].shape[0]
    heads = groups // 4
    state = args[5].shape[1] // 8
    band = tokens // n
    part = state // n
    flat = [v if v.ndim > 1 else v.reshape(1, -1) for v in args]
    flat[0] = region[0].T
    flat[6] = flat[6].T
    flat[11] = flat[11].T
    ent_rows = max(16, 2 * part)
    dma = pltpu.SemaphoreType.DMA
    vmem = pltpu.VMEM
    refined = pl.pallas_call(
        functools.partial(kernel, n, heads, state),
        out_shape=jax.ShapeDtypeStruct((width, tokens), BF),
        in_specs=[pl.BlockSpec(memory_space=pltpu.VMEM)] * len(flat),
        out_specs=pl.BlockSpec(memory_space=pltpu.VMEM),
        scratch_shapes=[
            vmem((2, width, tokens), BF),
            vmem((3, tokens + 16, inner), F32),
            vmem((tokens, inner), BF),
            vmem((n, band, inner), BF),
            vmem((n, band, inner), BF),
            vmem((tokens, inner), BF),
            vmem((tokens, inner), BF),
            vmem((tokens, inner), BF),
            vmem((2, tokens, 4 * state), BF),
            vmem((2, tokens, groups), F32),
            vmem((2, groups, tokens), F32),
            vmem((2, groups, tokens), F32),
            vmem((tokens, inner), F32),
            vmem((tokens, inner), F32),
            vmem((2, n, 2 * part, inner), F32),
            vmem((2, n, 2 * part, inner), F32),
            vmem((2, 8, 128), F32),
            vmem((2, n, 8, 128), F32),
            vmem((2, n, ent_rows, inner), BF),
            vmem((2, n, ent_rows, inner), BF),
            vmem((n, band, inner), BF),
            vmem((n, band, inner), BF),
            dma((2, tokens // TILE)),
            dma((2, tokens // TILE)),
            dma((n,)),
            dma((n,)),
            dma((2, n)),
            dma((2, n)),
            dma((2, n)),
            dma((2, n)),
            dma((2, n)),
            dma((2, n)),
            dma((n,)),
            dma((n,)),
        ],
        compiler_params=pltpu.CompilerParams(
            collective_id=0, has_side_effects=True, vmem_limit_bytes=50 * 1024 * 1024
        ),
    )(*flat)
    return refined.T[None]


def solution(mesh):
    in_specs = (P(("dp", "seq"), None, None),) + (P(),) * 11
    return jax.shard_map(
        functools.partial(body, mesh.shape["seq"]),
        mesh=mesh,
        in_specs=in_specs,
        out_specs=P(("dp", "seq"), None, None),
        check_vma=False,
    )
```

```python
import functools
import jax
import jax.numpy as jnp
from jax import lax
from jax.experimental import pallas as pl
from jax.experimental.pallas import tpu as pltpu
from jax.sharding import PartitionSpec as P

EPSILON = 1e-05
BF = jnp.bfloat16
F32 = jnp.float32
TILE = 128


def mm(a, b):
    return jnp.dot(a, b, preferred_element_type=F32)


def mm_nt(a, b):
    return lax.dot_general(a, b, (((1,), (1,)), ((), ())), preferred_element_type=F32)


def mm_tn(a, b):
    return lax.dot_general(a, b, (((0,), (0,)), ((), ())), preferred_element_type=F32)


def split3(v):
    hi = v.astype(BF)
    rest = v - hi.astype(F32)
    mid = rest.astype(BF)
    lo = (rest - mid.astype(F32)).astype(BF)
    return hi, mid, lo


def iota(shape, dim):
    return lax.broadcasted_iota(jnp.int32, shape, dim)


def kernel(
    n,
    heads,
    state,
    region_ref,
    norm_gain_ref,
    in_w_ref,
    conv_w_ref,
    conv_b_ref,
    coup_w_ref,
    step_w_ref,
    step_b_ref,
    decay_ref,
    skip_ref,
    out_gain_ref,
    out_w_ref,
    out_ref,
    halo,
    pre,
    gate,
    act,
    colbuf,
    xcol,
    xe,
    xo,
    coup,
    cum,
    cum_t,
    step_t,
    own_row,
    own_col,
    msg,
    got,
    tot,
    got_tot,
    ent_out,
    ent_in,
    col_out,
    col_in,
    halo_send,
    halo_recv,
    a_send,
    a_recv,
    s_send,
    s_recv,
    t_send,
    t_recv,
    e_send,
    e_recv,
    c_send,
    c_recv,
):
    me = lax.axis_index("seq")
    width, tokens = region_ref.shape
    inner = out_w_ref.shape[1]
    band = tokens // n
    head = inner // heads
    part = state // n
    head_bits = head.bit_length() - 1
    n_bits = n.bit_length() - 1
    band_bits = band.bit_length() - 1
    groups = 4 * heads

    def peer_of(k):
        return lax.rem(me + k, n)

    def source_of(k):
        return lax.rem(me + n - k, n)

    barrier = pltpu.get_barrier_semaphore()

    def greet(k, _):
        pl.semaphore_signal(barrier, inc=1, device_id={"seq": peer_of(k)})
        return 0

    lax.fori_loop(1, n, greet, 0)
    pl.semaphore_wait(barrier, n - 1)

    tiles = tokens // TILE

    def halo_copy(slot, c, device):
        cells = pl.ds(c * TILE, TILE)
        return pltpu.make_async_remote_copy(
            src_ref=region_ref.at[:, cells],
            dst_ref=halo.at[slot, :, cells],
            send_sem=halo_send.at[slot, c],
            recv_sem=halo_recv.at[slot, c],
            device_id={"seq": device},
        )

    for c in range(tiles):

        @pl.when(me < n - 1)
        def _(c=c):
            halo_copy(0, c, me + 1).start()

        @pl.when(me > 0)
        def _(c=c):
            halo_copy(1, c, me - 1).start()

    @pl.when(me == n - 1)
    def _():
        halo[1] = jnp.zeros((width, tokens), BF)

    @pl.when(me == 0)
    def _():
        halo[0] = jnp.zeros((width, tokens), BF)

    square = (width, width)
    gain_column = jnp.sum(
        jnp.where(iota(square, 0) == iota(square, 1), norm_gain_ref[...], 0.0), axis=1, keepdims=True
    )

    def normed(values):
        mean_square = jnp.mean(values * values, axis=0, keepdims=True)
        return (values * lax.rsqrt(mean_square + EPSILON) * gain_column).astype(BF)

    edge = jnp.zeros((8, inner), F32)
    for a in range(3):
        pre[a, 0:8, :] = edge
        pre[a, tokens + 8 : tokens + 16, :] = edge
    own = normed(region_ref[...].astype(F32))
    pre[1, 8 : tokens + 8, :] = mm_tn(own, in_w_ref[:, :inner]).astype(BF).astype(F32)

    def a_copy(k, chunk, place):
        return pltpu.make_async_remote_copy(
            src_ref=act.at[chunk],
            dst_ref=colbuf.at[place],
            send_sem=a_send.at[k],
            recv_sem=a_recv.at[k],
            device_id={"seq": chunk},
        )

    per = TILE // band if band < TILE else 1
    def convolve(c):
        summed = conv_b_ref[...]
        for a in range(3):
            for b in range(3):
                first = c * TILE + 7 + b
                tap = 3 * a + b
                summed = summed + pre[a, first : first + TILE, :] * conv_w_ref[tap : tap + 1, :]
        done = (summed / (1.0 + jnp.exp(-summed))).astype(BF)
        if band <= TILE:
            act[c * per : (c + 1) * per] = done.reshape(per, band, inner)
        else:
            where = c * TILE // band
            start = c * TILE % band
            act[where, start : start + TILE] = done
        for d in range(c * TILE // band, (c + 1) * TILE // band):

            @pl.when(me != d)
            def _(d=d):
                a_copy(lax.rem(d - me + n, n), d, me).start()


    for c in range(tiles + 1):
        if c < tiles:

            @pl.when(me < n - 1)
            def _(c=c):
                halo_copy(1, c, me + 1).wait_recv()

            @pl.when(me > 0)
            def _(c=c):
                halo_copy(0, c, me - 1).wait_recv()

            cells = slice(c * TILE, (c + 1) * TILE)
            for slot, a in ((0, 0), (1, 2)):
                rim = mm_tn(normed(halo[slot, :, cells].astype(F32)), in_w_ref[:, :inner])
                pre[a, 8 + c * TILE : 8 + (c + 1) * TILE, :] = rim.astype(BF).astype(F32)
        if c > 0:
            convolve(c - 1)

    gate[...] = mm_tn(own, in_w_ref[:, inner:]).astype(BF)

    def s_copy(p, k, chunk, place):
        return pltpu.make_async_remote_copy(
            src_ref=msg.at[p, chunk],
            dst_ref=got.at[p, place],
            send_sem=s_send.at[p, k],
            recv_sem=s_recv.at[p, k],
            device_id={"seq": chunk},
        )

    def t_copy(p, k, chunk, place):
        return pltpu.make_async_remote_copy(
            src_ref=tot.at[p],
            dst_ref=got_tot.at[p, place],
            send_sem=t_send.at[p, k],
            recv_sem=t_recv.at[p, k],
            device_id={"seq": chunk},
        )

    def e_copy(p, k, chunk, place):
        return pltpu.make_async_remote_copy(
            src_ref=ent_out.at[p, chunk],
            dst_ref=ent_in.at[p, place],
            send_sem=e_send.at[p, k],
            recv_sem=e_recv.at[p, k],
            device_id={"seq": chunk},
        )

    def c_copy(k, chunk, place):
        return pltpu.make_async_remote_copy(
            src_ref=col_out.at[chunk],
            dst_ref=col_in.at[place],
            send_sem=c_send.at[k],
            recv_sem=c_recv.at[k],
            device_id={"seq": chunk},
        )

    def start_all(make):
        def one(k, _):
            make(k, peer_of(k), me).start()
            return 0

        lax.fori_loop(1, n, one, 0)

    def wait_all(make):
        def one(k, _):
            make(k, peer_of(k), source_of(k)).wait_recv()
            return 0

        lax.fori_loop(1, n, one, 0)

    def wait_sent(make):
        def one(k, _):
            make(k, peer_of(k), source_of(k)).wait_send()
            return 0

        lax.fori_loop(1, n, one, 0)

    colbuf[pl.ds(me, 1)] = act[pl.ds(me, 1)]

    group_lane = iota((1, groups), 1)
    behind_lane = lax.rem(group_lane, 2 * heads) >= heads
    lower = (iota((tokens, tokens), 0) >= iota((tokens, tokens), 1)).astype(BF)
    eye = (iota((groups, groups), 0) == iota((groups, groups), 1)).astype(BF)
    spread_row = iota((groups, inner), 0)
    spread_head = jnp.right_shift(iota((groups, inner), 1), head_bits)
    rates = -jnp.exp(decay_ref[...])

    def spreader(base):
        return (spread_row == base + spread_head).astype(F32)

    def expand(v, e):
        hi, mid, lo = (piece.astype(F32) for piece in split3(v))
        pieces = jnp.concatenate([hi, mid, lo], axis=1).astype(BF)
        return mm(pieces, jnp.concatenate([e, e, e], axis=0).astype(BF))

    def flip_axes(v):
        hi, mid, lo = split3(v)
        return mm_nt(eye, hi) + mm_nt(eye, mid) + mm_nt(eye, lo)

    def prepare(p, x):
        first = p * 4 * state
        coup[p] = mm(x, coup_w_ref[:, first : first + 4 * state]).astype(BF)
        logits = mm_nt(x, step_w_ref[...]) + step_b_ref[...]
        steps = jnp.maximum(logits, 0.0) + jnp.log1p(jnp.exp(-jnp.abs(logits)))
        logs = rates * steps
        hi, mid, lo = split3(logs)
        ahead = mm(lower, hi) + mm(lower, mid) + mm(lower, lo)
        total = ahead[tokens - 1 : tokens, :]
        c = jnp.where(behind_lane, total - ahead + logs, ahead)
        cum[p] = c
        tail = jnp.exp(total - c) * steps
        base = p * 2 * heads
        xf = x.astype(F32)
        spread_a, spread_b = spreader(base), spreader(base + heads)
        tot[p, :, 0:groups] = jnp.broadcast_to(total, (8, groups))
        start_all(functools.partial(t_copy, p))
        got_tot[p, pl.ds(me, 1)] = tot[p][None]
        contribs = []
        for o, e in ((0, spread_a), (1, spread_b)):
            weighted = (xf * expand(tail, e)).astype(BF)
            writer = coup[p, :, 2 * o * state : (2 * o + 1) * state]
            contribs.append(mm_tn(writer, weighted))
        for d in range(n):
            for o in range(2):
                msg[p, d, o * part : (o + 1) * part] = contribs[o][d * part : (d + 1) * part]
        if p == 1:
            start_all(functools.partial(s_copy, p))
        cum_t[p] = flip_axes(c)
        step_t[p] = flip_axes(steps)
        got[p, pl.ds(me, 1)] = msg[p, pl.ds(me, 1)]
        def diagonal(o):
            w = coup[p, :, 2 * o * state : (2 * o + 1) * state].astype(F32)
            r = coup[p, :, (2 * o + 1) * state : (2 * o + 2) * state].astype(F32)
            return jnp.sum(w * r, axis=-1, keepdims=True)

        diag = (jnp.where(behind_lane, diagonal(1), diagonal(0)) * steps).astype(BF).astype(F32)
        target = own_col if p else own_row
        target[...] = xf * expand(diag + skip_ref[...], spread_a + spread_b)
        even = jnp.bitwise_and(iota((1, inner), 1), head) == 0
        xe[...] = jnp.where(even, xf, 0.0).astype(BF)
        xo[...] = jnp.where(even, 0.0, xf).astype(BF)

    def mix(p, first, last):
        target = own_col if p else own_row

        def tile(i, _):
            t0 = pl.multiple_of(i * TILE, TILE)
            rows = pl.ds(t0, TILE)
            both = coup[p, rows, :]
            ahead = mm_nt(both[:, state : 2 * state], coup[p, :, 0:state])
            behind = mm_nt(both[:, 3 * state : 4 * state], coup[p, :, 2 * state : 3 * state])
            t = iota((TILE, tokens), 0) + t0
            s = iota((TILE, tokens), 1)
            after = t > s
            scores = jnp.where(after, ahead, jnp.where(t < s, behind, 0.0))
            c = cum[p, rows, :]

            def weights(h):
                f = p * 2 * heads + h
                g = f + heads
                lead = c[:, f : f + 1] - cum_t[p, f : f + 1, :]
                back = c[:, g : g + 1] - cum_t[p, g : g + 1, :]
                step = jnp.where(after, step_t[p, f : f + 1, :], step_t[p, g : g + 1, :])
                return (scores * jnp.exp(jnp.minimum(lead, back)) * step).astype(BF)

            for j in range(heads // 2):
                lanes = slice(2 * j * head, 2 * (j + 1) * head)
                inside = mm(weights(2 * j), xe[:, lanes]) + mm(weights(2 * j + 1), xo[:, lanes])
                target[rows, lanes] += inside
            return 0

        lax.fori_loop(first, last, tile, 0)

    def scan(p):
        wait_all(functools.partial(t_copy, p))
        base = p * 2 * heads
        totals = jnp.exp(
            jnp.concatenate([got_tot[p, i, 0:8, 0:groups] for i in range(n)], axis=0)
        )
        fade_a = expand(totals, spreader(base))
        fade_b = expand(totals, spreader(base + heads))
        wait_all(functools.partial(s_copy, p))
        entry = jnp.zeros((part, inner), F32)
        ahead = []
        for i in range(n):
            ahead.append(entry)
            entry = fade_a[8 * i : 8 * i + 1] * entry + got[p, i, 0:part, :]
        entry = jnp.zeros((part, inner), F32)
        for i in reversed(range(n)):
            pieces = [ahead[i], entry]
            if 2 * part < 16:
                pieces.append(jnp.zeros((16 - 2 * part, inner), F32))
            ent_out[p, i] = jnp.concatenate(pieces, axis=0).astype(BF)
            entry = fade_b[8 * i : 8 * i + 1] * entry + got[p, i, part : 2 * part, :]
        start_all(functools.partial(e_copy, p))
        ent_in[p, pl.ds(me, 1)] = ent_out[p, pl.ds(me, 1)]

    def finish(p):
        wait_all(functools.partial(e_copy, p))
        target = own_col if p else own_row
        arrived = [ent_in[p, i].astype(F32) for i in range(n)]
        grown = jnp.exp(cum[p])
        base = p * 2 * heads
        result = target[...]
        for o in range(2):
            entry = jnp.concatenate(
                [v[o * part : (o + 1) * part] for v in arrived], axis=0
            ).astype(BF)
            reader = coup[p, :, (2 * o + 1) * state : (2 * o + 2) * state]
            result = result + mm(reader, entry) * expand(grown, spreader(base + o * heads))
        return result

    x_row = act[...].reshape(tokens, inner)
    prepare(0, x_row)
    mix(0, 0, tiles)
    wait_all(a_copy)
    start_all(functools.partial(s_copy, 0))
    place = iota((tokens, tokens), 0)
    cell = iota((tokens, tokens), 1)
    turn = cell == jnp.left_shift(jnp.bitwise_and(place, n - 1), band_bits) + jnp.right_shift(place, n_bits)
    xcol[...] = mm(turn.astype(BF), colbuf[...].reshape(tokens, inner)).astype(BF)
    prepare(1, xcol[...])
    mix(1, 0, tiles // 2)
    scan(1)
    scan(0)
    mix(1, tiles // 2, tiles)
    column = finish(1).astype(BF)
    back = cell == jnp.left_shift(jnp.bitwise_and(place, band - 1), n_bits) + jnp.right_shift(place, band_bits)
    back = back.astype(BF)
    for d in range(n):
        col_out[d] = mm(back[d * band : (d + 1) * band], column).astype(BF)

        @pl.when(me != d)
        def _(d=d):
            c_copy(lax.rem(d - me + n, n), d, me).start()

    col_in[pl.ds(me, 1)] = col_out[pl.ds(me, 1)]
    row_total = finish(0)
    g = gate[...].astype(F32)
    own_row[...] = row_total
    own_col[...] = g / (1.0 + jnp.exp(-g))
    wait_all(c_copy)
    for c in range(tokens // TILE):
        rows = slice(c * TILE, (c + 1) * TILE)
        if band <= TILE:
            col = col_in[c * per : (c + 1) * per].reshape(TILE, inner)
        else:
            start = c * TILE % band
            col = col_in[c * TILE // band, start : start + TILE]
        gated = (own_row[rows, :] + col.astype(F32)) * own_col[rows, :]
        mean_square = jnp.mean(gated * gated, axis=-1, keepdims=True)
        normy = (gated * lax.rsqrt(mean_square + EPSILON) * out_gain_ref[...]).astype(BF)
        out_ref[:, rows] = (
            region_ref[:, rows].astype(F32) + mm_nt(out_w_ref[...], normy)
        ).astype(BF)
    for c in range(tiles):

        @pl.when(me < n - 1)
        def _(c=c):
            halo_copy(0, c, me + 1).wait_send()

        @pl.when(me > 0)
        def _(c=c):
            halo_copy(1, c, me - 1).wait_send()

    wait_sent(a_copy)
    for p in range(2):
        wait_sent(functools.partial(s_copy, p))
        wait_sent(functools.partial(t_copy, p))
        wait_sent(functools.partial(e_copy, p))
    wait_sent(c_copy)


def body(n, *args):
    region = args[0]
    rows, tokens, width = region.shape
    inner = args[11].shape[0]
    groups = args[7].shape[0]
    heads = groups // 4
    state = args[5].shape[1] // 8
    band = tokens // n
    part = state // n
    flat = [v if v.ndim > 1 else v.reshape(1, -1) for v in args]
    flat[0] = region[0].T
    flat[6] = flat[6].T
    flat[11] = flat[11].T
    ent_rows = max(16, 2 * part)
    dma = pltpu.SemaphoreType.DMA
    vmem = pltpu.VMEM
    refined = pl.pallas_call(
        functools.partial(kernel, n, heads, state),
        out_shape=jax.ShapeDtypeStruct((width, tokens), BF),
        in_specs=[pl.BlockSpec(memory_space=pltpu.VMEM)] * len(flat),
        out_specs=pl.BlockSpec(memory_space=pltpu.VMEM),
        scratch_shapes=[
            vmem((2, width, tokens), BF),
            vmem((3, tokens + 16, inner), F32),
            vmem((tokens, inner), BF),
            vmem((n, band, inner), BF),
            vmem((n, band, inner), BF),
            vmem((tokens, inner), BF),
            vmem((tokens, inner), BF),
            vmem((tokens, inner), BF),
            vmem((2, tokens, 4 * state), BF),
            vmem((2, tokens, groups), F32),
            vmem((2, groups, tokens), F32),
            vmem((2, groups, tokens), F32),
            vmem((tokens, inner), F32),
            vmem((tokens, inner), F32),
            vmem((2, n, 2 * part, inner), F32),
            vmem((2, n, 2 * part, inner), F32),
            vmem((2, 8, 128), F32),
            vmem((2, n, 8, 128), F32),
            vmem((2, n, ent_rows, inner), BF),
            vmem((2, n, ent_rows, inner), BF),
            vmem((n, band, inner), BF),
            vmem((n, band, inner), BF),
            dma((2, tokens // TILE)),
            dma((2, tokens // TILE)),
            dma((n,)),
            dma((n,)),
            dma((2, n)),
            dma((2, n)),
            dma((2, n)),
            dma((2, n)),
            dma((2, n)),
            dma((2, n)),
            dma((n,)),
            dma((n,)),
        ],
        compiler_params=pltpu.CompilerParams(
            collective_id=0, has_side_effects=True, vmem_limit_bytes=50 * 1024 * 1024
        ),
    )(*flat)
    return refined.T[None]


def solution(mesh):
    in_specs = (P(("dp", "seq"), None, None),) + (P(),) * 11
    return jax.shard_map(
        functools.partial(body, mesh.shape["seq"]),
        mesh=mesh,
        in_specs=in_specs,
        out_specs=P(("dp", "seq"), None, None),
        check_vma=False,
    )
```
